128 devices in a mesh: fs: 32 (over z, x, core), pol: 4 (over y).
Axes of the slice: x: 4, y: 4, z: 4, core: 2. Of those that a mesh axis runs over, the one named last changes fastest.
Arguments:
- facets: bfloat16 [4, 64, 4096, 128], P('pol', 'fs'), may hold values from -6 to 6
- owners: int32 [64], replicated, may hold values from 0 to 31, as said below
- counts: int32 [64], replicated, may hold values from 1 to 8, as said below
- coords: float32 [2, 128, 8, 128], P(None, 'fs'), may hold values from 0 to 512
- station_ids: int32 [128, 8, 2, 128], P('fs'), may hold values from 0 to 511
- jones_table: float32 [8, 512], replicated, may hold values from -3 to 3
Outputs:
- predicted: float32 [4, 2, 128, 8, 128], P('pol', None, 'fs')
The draws below stay inside these ranges and needn't reach their ends.
Inputs may be any that keep to these rules, and one draw needn't show every extreme that they name: `owners`: each fs index owns at most 4 subgrids, and some index owns exactly 4. `counts`: some subgrid has exactly 8 blocks.
All inputs are finite; a program needn't handle non-finite values.
Results may differ from the reference program's by a relative error of at most 0.0055.
Values may be sent and summed in bfloat16 or wider, within the bound.
No kernel may reach another device: no remote copies, remote signals or barrier semaphores. Data moves between devices by JAX's collectives and lax.ppermute only.
A program may use at most 64 MiB of HBM per device.

```python
import math
import jax
import jax.numpy as jnp
from jax import lax

R = 8
W = 64
S = 64
MAXB = 8
VB = 128
NST = 512
POLS = 4
F = 64
FH = 4096
SG = 512
CAP = 4
SLOTS = 128
N_FS = 32


def draw_owners(key, part):
    device_count = 2 * S // CAP
    base_load = CAP // 2
    key_order, key_shift, key_mix = jax.random.split(jax.random.fold_in(key, 11), 3)
    ordering = jax.random.permutation(key_order, device_count)
    shifts = jax.random.randint(key_shift, (device_count // 2,), 0, base_load + 1)
    shifts = shifts.at[0].set(base_load)
    device_loads = jnp.zeros((device_count,), jnp.int32)
    device_loads = device_loads.at[ordering[0::2]].set(base_load + shifts)
    device_loads = device_loads.at[ordering[1::2]].set(base_load - shifts)
    holders = jnp.repeat(jnp.arange(device_count, dtype=jnp.int32), device_loads, total_repeat_length=S)
    return holders[jax.random.permutation(key_mix, S)].astype(jnp.int32)


def draw_counts(key, part):
    key_values, key_place = jax.random.split(jax.random.fold_in(key, 23), 2)
    values = jax.random.randint(key_values, (S,), 1, MAXB + 1)
    position = jax.random.randint(key_place, (), 0, S)
    return values.at[position].set(MAXB).astype(jnp.int32)


def set_ends(entries, stream_key, least, largest):
    longest = entries.shape.index(max(entries.shape))
    spots = []
    for shift in (0, 1):
        where = [jax.random.randint(jax.random.fold_in(stream_key, axis), (), 0, length) for axis, length in enumerate(entries.shape)]
        where[longest] = (where[longest] + shift) % entries.shape[longest]
        spots.append(tuple(where))
    return entries.at[spots[0]].set(least).at[spots[1]].set(largest)


def block_scale(rng, shape, cuts, low, high):
    def one(axis_at, blocks):
        steps = jax.random.uniform(jax.random.fold_in(jax.random.fold_in(rng, 6), axis_at), (blocks,), jnp.float32, low / len(cuts), high / len(cuts))
        return jnp.repeat(jnp.exp(steps), shape[axis_at] // blocks).reshape((-1,) + (1,) * (len(shape) - axis_at - 1))

    gain = one(*cuts[0])
    for cut in cuts[1:]:
        gain = gain * one(*cut)
    return gain


def bell_draw(key, shape, deviation, bound, shards=(), held_as=jnp.bfloat16):
    entries = jax.random.normal(key, shape, jnp.float32) * deviation
    if len(shards) > 0:
        entries = block_scale(key, shape, shards, -0.22, 0.18) * entries
    return jnp.clip(entries, min=-bound, max=bound).astype(held_as)


def setup_inputs(seed: int = 0) -> dict:
    keys = jax.random.split(jax.random.key(seed), 7)
    facets = bell_draw(keys[0], (POLS, F, FH, 2 * W), 1.0, 6.0, ((0, 4), (1, 32)))
    owners = draw_owners(jax.random.fold_in(keys[6], 71), 0)
    counts = draw_counts(jax.random.fold_in(keys[6], 71), 0)
    coords = jnp.clip(512.0 * jax.random.uniform(keys[3], (2, SLOTS, MAXB, VB), jnp.float32) ** block_scale(keys[3], (2, SLOTS, MAXB, VB), ((1, 32),), -0.2, 0.2), 0.0, 512.0)
    station_ids = set_ends(jax.random.randint(keys[4], (SLOTS, MAXB, 2, VB), 0, NST), jax.random.fold_in(keys[4], 1), 0, NST - 1).astype(jnp.int32)
    jones_table = bell_draw(keys[5], (8, NST), 0.5, 3.0, (), jnp.float32)
    return dict(facets=facets, owners=owners, counts=counts, coords=coords, station_ids=station_ids, jones_table=jones_table)


def dft_tables(length):
    indices = jnp.arange(length, dtype=jnp.int32)
    phases = indices[:, None] * indices[None, :] % length
    angles = phases.astype(jnp.float32) * (2.0 * math.pi / length)
    return (jnp.cos(angles).astype(jnp.bfloat16), jnp.sin(angles).astype(jnp.bfloat16))

def turn_table(rows, cols, length):
    row_index = jnp.arange(rows, dtype=jnp.int32)
    col_index = jnp.arange(cols, dtype=jnp.int32)
    phases = row_index[:, None] * col_index[None, :] % length
    angles = phases.astype(jnp.float32) * (2.0 * math.pi / length)
    return (jnp.cos(angles), jnp.sin(angles))

def cell_phases(positions, cells):
    offsets = jnp.arange(cells, dtype=jnp.float32) - cells // 2
    angles = jnp.mod(positions[:, None] * offsets[None, :], float(cells)) * (2.0 * math.pi / cells)
    return (jnp.cos(angles), jnp.sin(angles))

def complex_product(left_real, left_imag, right_real, right_imag):
    return (left_real * right_real - left_imag * right_imag, left_real * right_imag + left_imag * right_real)

def reference(facets, owners, counts, coords, station_ids, jones_table):
    first_cos, first_sin = dft_tables(W)
    second_cos, second_sin = dft_tables(S)
    turn_cos, turn_sin = turn_table(W, S, FH)
    scale = 1.0 / math.sqrt(FH)
    flat_strips = facets.reshape(POLS * F, W, S, 2 * W)

    def transform(strip):
        cos_part = jnp.einsum('kn,nmc->kmc', first_cos, strip, preferred_element_type=jnp.float32)
        sin_part = jnp.einsum('kn,nmc->kmc', first_sin, strip, preferred_element_type=jnp.float32)
        section_real = cos_part[..., :W] + sin_part[..., W:]
        section_imag = cos_part[..., W:] - sin_part[..., :W]
        tc = turn_cos[:, :, None]
        ts = turn_sin[:, :, None]
        turned = jnp.concatenate([section_real * tc + section_imag * ts, section_imag * tc - section_real * ts], axis=2).astype(jnp.bfloat16)
        cos_two = jnp.einsum('qm,kmc->qkc', second_cos, turned, preferred_element_type=jnp.float32)
        sin_two = jnp.einsum('qm,kmc->qkc', second_sin, turned, preferred_element_type=jnp.float32)
        real_part = (cos_two[..., :W] + sin_two[..., W:]) * scale
        imag_part = (cos_two[..., W:] - sin_two[..., :W]) * scale
        return jnp.concatenate([real_part, imag_part], axis=2).reshape(FH, 2 * W).astype(jnp.bfloat16)
    windows = lax.map(transform, flat_strips).reshape(POLS, F, FH, 2 * W)
    owned = (owners[None, :] == jnp.arange(N_FS, dtype=jnp.int32)[:, None]).astype(jnp.int32)
    ranks = jnp.cumsum(owned, axis=1) - 1
    rank_of = lax.optimization_barrier(jnp.sum(owned * ranks, axis=0))
    slot_of = owners * CAP + rank_of

    def predict(index):
        tile = lax.dynamic_slice_in_dim(windows, index * W, W, axis=2)
        real_grid = tile[..., :W].reshape(POLS, R, R, W, W).transpose(0, 1, 3, 2, 4).reshape(POLS, SG, SG)
        imag_grid = tile[..., W:].reshape(POLS, R, R, W, W).transpose(0, 1, 3, 2, 4).reshape(POLS, SG, SG)
        grids = jnp.concatenate([real_grid, imag_grid], axis=2)
        positions = lax.dynamic_index_in_dim(coords, slot_of[index], axis=1, keepdims=False)
        row_cos, row_sin = cell_phases(positions[0].reshape(-1), SG)
        row_cos = row_cos.astype(jnp.bfloat16)
        row_sin = row_sin.astype(jnp.bfloat16)
        col_cos, col_sin = cell_phases(positions[1].reshape(-1), SG)
        results = []
        for pol_index in range(POLS):
            cos_part = jnp.dot(row_cos, grids[pol_index], preferred_element_type=jnp.float32)
            sin_part = jnp.dot(row_sin, grids[pol_index], preferred_element_type=jnp.float32)
            real_part = cos_part[:, :SG] + sin_part[:, SG:]
            imag_part = cos_part[:, SG:] - sin_part[:, :SG]
            vis_real = lax.optimization_barrier(jnp.sum(real_part * col_cos + imag_part * col_sin, axis=1)) / SG
            vis_imag = lax.optimization_barrier(jnp.sum(imag_part * col_cos - real_part * col_sin, axis=1)) / SG
            results.append(jnp.stack([vis_real, vis_imag]).reshape(2, MAXB, VB))
        return jnp.stack(results)
    per_subgrid = lax.map(predict, jnp.arange(S, dtype=jnp.int32))
    matches = owned[:, :, None] * (ranks[:, :, None] == jnp.arange(CAP, dtype=jnp.int32)[None, None, :]).astype(jnp.int32)
    slot_subgrid = lax.optimization_barrier(jnp.sum(matches * jnp.arange(S, dtype=jnp.int32)[None, :, None], axis=1)).reshape(-1)
    slot_valid = lax.optimization_barrier(jnp.sum(matches, axis=1)).reshape(-1)
    visible = jnp.take(per_subgrid, slot_subgrid, axis=0)
    block_limit = jnp.take(counts, slot_subgrid) * slot_valid
    keep = jnp.arange(MAXB, dtype=jnp.int32)[None, :] < block_limit[:, None]
    left = jnp.take(jones_table, station_ids[:, :, 0, :], axis=1)
    right = jnp.take(jones_table, station_ids[:, :, 1, :], axis=1)
    outputs = []
    for row_side in range(2):
        for col_side in range(2):
            total_real = jnp.zeros(visible.shape[:1] + visible.shape[3:], jnp.float32)
            total_imag = jnp.zeros(visible.shape[:1] + visible.shape[3:], jnp.float32)
            for inner_row in range(2):
                for inner_col in range(2):
                    left_entry = 2 * (2 * row_side + inner_row)
                    right_entry = 2 * (2 * col_side + inner_col)
                    comp_real = visible[:, 2 * inner_row + inner_col, 0]
                    comp_imag = visible[:, 2 * inner_row + inner_col, 1]
                    step_real, step_imag = complex_product(left[left_entry], left[left_entry + 1], comp_real, comp_imag)
                    step_real, step_imag = complex_product(step_real, step_imag, right[right_entry], -right[right_entry + 1])
                    total_real = total_real + step_real
                    total_imag = total_imag + step_imag
            outputs.append(jnp.stack([total_real, total_imag]))
    corrected = jnp.stack(outputs)
    return jnp.where(keep[None, None, :, :, None], corrected, 0.0)
```

```python
import math

import jax
import jax.numpy as jnp
import numpy as np
from jax import lax
from jax.experimental import pallas as pl
from jax.experimental.pallas import tpu as pltpu
from jax.sharding import PartitionSpec as P

R = 8
W = 64
S = 64
MAXB = 8
VB = 128
FH = 4096
SG = 512
CAP = 4
UNITS = 256
VMEM_LIMIT = 48 * 1024 * 1024
F32 = jnp.float32
BF16 = jnp.bfloat16


def first_table():
    index = np.arange(W)
    angles = (index[:, None] * index[None, :] % W) * (2.0 * math.pi / W)
    return np.concatenate([np.cos(angles), np.sin(angles)], axis=0).astype(BF16)


def second_table():
    k1 = np.arange(W)[:, None, None]
    k2 = np.arange(S)[None, :, None]
    n1 = np.arange(W)[None, None, :]
    angles = (n1 * (k1 + W * k2) % FH) * (2.0 * math.pi / FH)
    cos, sin = np.cos(angles), np.sin(angles)
    upper = np.concatenate([cos, -sin], axis=2)
    lower = np.concatenate([sin, cos], axis=2)
    return np.concatenate([upper, lower], axis=1).astype(BF16)


def mirror_table():
    table = np.zeros((2 * W, 2 * W), np.float32)
    index = np.arange(W)
    table[W - 1 - index, index] = 1.0
    table[2 * W - 1 - index, W + index] = 1.0
    return table.astype(BF16)


SIN_TERMS = (3.14159264, -5.16771008, 2.55007752, -0.598291286, 0.0776576603)
COS_TERMS = (0.999999953, -4.93479283, 4.05841135, -1.33187657, 0.219689611)


def polynomial(terms, x):
    total = jnp.full_like(x, terms[-1])
    for term in terms[-2::-1]:
        total = total * x + term
    return total


def turns_to_phase(turns):
    part = turns - jnp.round(turns)
    square = part * part
    half_sin = part * polynomial(SIN_TERMS, square)
    half_cos = polynomial(COS_TERMS, square)
    twice = half_sin + half_sin
    return (1.0 - twice * half_sin, twice * half_cos)


def rotate(cos, sin, step_cos, step_sin):
    return (cos * step_cos - sin * step_sin, sin * step_cos + cos * step_sin)


def transform_kernel(facets_ref, first_ref, second_ref, mirror_ref, out_ref, rows, sections, mixed):
    mirror = mirror_ref[...]
    piece = 512

    @pl.loop(0, FH // piece)
    def _(step):
        at = pl.ds(pl.multiple_of(step * piece, piece), piece)
        rows[0, at, :] = jnp.dot(facets_ref[0, at, :], mirror, preferred_element_type=F32)
        rows[1, at, :] = facets_ref[1, at, :].astype(F32)

    first = first_ref[...]

    @pl.loop(0, W // 8)
    def _(step):
        for inner in range(8):
            n1 = step * 8 + inner
            strip = jnp.concatenate([rows[f, pl.ds(n1, W, stride=W), :] for f in range(2)], axis=1)
            part = jnp.dot(first, strip.astype(BF16), preferred_element_type=F32)
            for f in range(2):
                lanes = slice(2 * W * f, 2 * W * (f + 1))
                sections[f, pl.ds(n1, W, stride=2 * W), :] = part[:W, lanes]
                sections[f, pl.ds(W + n1, W, stride=2 * W), :] = part[W:, lanes]

    low_lanes = lax.broadcasted_iota(jnp.int32, (S, 2 * W), 1) < W

    def window(k1):
        at = pl.ds(pl.multiple_of(k1 * 2 * W, 2 * W), 2 * W)
        section = jnp.concatenate([sections[f, at, :] for f in range(2)], axis=1).astype(BF16)
        return jnp.dot(second_ref[k1], section, preferred_element_type=F32)

    @pl.loop(0, W // 4)
    def _(step):
        for inner in range(2):
            index = step * 2 + inner
            above = window(W // 2 + index)
            below = window(W // 2 - 1 - index)
            for half, grid in enumerate((above + below, above - below)):
                cos_0, cos_1 = grid[:S, : 2 * W], grid[:S, 2 * W :]
                sin_0, sin_1 = grid[S:, : 2 * W], grid[S:, 2 * W :]
                cos_sum, cos_gap = cos_1 + cos_0, cos_1 - cos_0
                sin_sum, sin_gap = sin_1 + sin_0, sin_1 - sin_0
                real = jnp.where(low_lanes, cos_sum, cos_gap) + pltpu.roll(
                    jnp.where(low_lanes, -sin_gap, sin_sum), W, 1
                )
                imag = pltpu.roll(jnp.where(low_lanes, -cos_gap, cos_sum), W, 1) - jnp.where(
                    low_lanes, sin_sum, sin_gap
                )
                mixed[pl.ds(64 * half + index, S, stride=2 * W), :] = real
                mixed[pl.ds(64 * half + 32 + index, S, stride=2 * W), :] = imag

    @pl.loop(0, S // 4)
    def _(step):
        for inner in range(4):
            s = step * 4 + inner
            at = pl.ds(pl.multiple_of(s * 2 * W, 2 * W), 2 * W)
            out_ref[s] = mixed[at, :].astype(BF16)


def transform(strips):
    return pl.pallas_call(
        transform_kernel,
        out_shape=jax.ShapeDtypeStruct((S, 2 * W, 2 * W), BF16),
        in_specs=[pl.BlockSpec(memory_space=pltpu.VMEM)] * 4,
        out_specs=pl.BlockSpec(memory_space=pltpu.VMEM),
        scratch_shapes=[
            pltpu.VMEM((2, FH, 2 * W), F32),
            pltpu.VMEM((2, 2 * FH, 2 * W), F32),
            pltpu.VMEM((2 * FH, 2 * W), F32),
        ],
        compiler_params=pltpu.CompilerParams(vmem_limit_bytes=VMEM_LIMIT),
        cost_estimate=pl.CostEstimate(flops=1_000_000_000, bytes_accessed=8_000_000, transcendentals=0),
    )(strips, jnp.asarray(first_table()), jnp.asarray(second_table()), jnp.asarray(mirror_table()))


def degrid_kernel(units, total, limits, centres, own_ref, other_ref, coords_ref, out_ref, steps, sums):
    @pl.loop(0, 16)
    def _(o):
        for c in range(CAP):
            for axis in range(2):
                cos, sin = turns_to_phase(coords_ref[o, axis, c] * (8.0 / SG))
                steps[2 * axis, o * CAP + c] = cos
                steps[2 * axis + 1, o * CAP + c] = sin

    cells = (lax.broadcasted_iota(jnp.int32, (8, VB), 0).astype(F32) + 0.5) * (1.0 / SG)

    def ladder(position, step_cos, step_sin, count):
        cos, sin = turns_to_phase(position * cells)
        both = [(cos, sin)]
        step_cos = jnp.broadcast_to(step_cos, (8, VB))
        step_sin = jnp.broadcast_to(step_sin, (8, VB))
        for _ in range(count - 1):
            cos, sin = rotate(cos, sin, step_cos, step_sin)
            both.append((cos, sin))
        return both

    def unit(index):
        word = units[index]
        pair = word % 4
        s = (word // 4) % S
        g = word // (4 * S)
        o, c = g // CAP, g % CAP
        phases, weights = [], []
        for h in range(2):
            b = 2 * pair + h
            row = pl.ds(b, 1)
            along_y = ladder(coords_ref[o, 1, c, row, :], steps[2, g, row, :], steps[3, g, row, :], 8)
            phases.append(jnp.concatenate([t[0] for t in along_y] + [t[1] for t in along_y], axis=0).astype(BF16))
            weights.append(ladder(coords_ref[o, 0, c, row, :], steps[0, g, row, :], steps[1, g, row, :], 4))
        phases = jnp.concatenate(phases, axis=1)
        both = jnp.concatenate([own_ref[s], other_ref[s]], axis=0)
        grid = jnp.dot(both, phases, preferred_element_type=F32)
        for h in range(2):
            b = 2 * pair + h
            lanes = slice(VB * h, VB * (h + 1))
            for q in range(2):
                real = imag = None
                for i, (cos, sin) in enumerate(weights[h]):
                    at = 128 * q + 8 * i
                    sum_real, sum_imag = grid[at : at + 8, lanes], grid[at + 32 : at + 40, lanes]
                    gap_real, gap_imag = grid[at + 64 : at + 72, lanes], grid[at + 96 : at + 104, lanes]
                    step_real = cos * sum_real + sin * gap_imag
                    step_imag = cos * sum_imag - sin * gap_real
                    real = step_real if real is None else real + step_real
                    imag = step_imag if imag is None else imag + step_imag
                at = pl.ds(pl.multiple_of(8 * b, 8), 8)
                sums[4 * g + 2 * q, at, :] = real
                sums[4 * g + 2 * q + 1, at, :] = imag

    @pl.loop(0, total[0])
    def _(index):
        unit(index)

    centre_x, centre_own, centre_other = centres[0], centres[1], centres[2]

    @pl.loop(0, 16 * CAP)
    def _(g):
        o, c = g // CAP, g % CAP

        @pl.when(limits[g] > 0)
        def _():
            x, y = coords_ref[o, 0, c], coords_ref[o, 1, c]
            real = imag = jnp.zeros((MAXB, VB), F32)
            for q, centre_y in enumerate((centre_own, centre_other)):
                total_real = sums[4 * g + 2 * q, pl.ds(0, MAXB, stride=8), :]
                total_imag = sums[4 * g + 2 * q + 1, pl.ds(0, MAXB, stride=8), :]
                for r in range(1, 8):
                    total_real = total_real + sums[4 * g + 2 * q, pl.ds(r, MAXB, stride=8), :]
                    total_imag = total_imag + sums[4 * g + 2 * q + 1, pl.ds(r, MAXB, stride=8), :]
                cos, sin = turns_to_phase((x * centre_x + y * centre_y) * (1.0 / SG))
                real = real + (cos * total_real + sin * total_imag)
                imag = imag + (cos * total_imag - sin * total_real)
            scale = 1.0 / (math.sqrt(FH) * SG)
            value = (jnp.concatenate([real, imag], axis=0) * scale).astype(BF16)
            for copy in range(4):
                out_ref[o, copy, c] = value


def degrid(units, total, limits, centres, own, other, coords):
    smem = pl.BlockSpec(memory_space=pltpu.SMEM)
    vmem = pl.BlockSpec(memory_space=pltpu.VMEM)
    return pl.pallas_call(
        degrid_kernel,
        out_shape=jax.ShapeDtypeStruct((16, 4, CAP, 2 * MAXB, VB), BF16),
        in_specs=[smem] * 4 + [vmem] * 3,
        out_specs=vmem,
        scratch_shapes=[
            pltpu.VMEM((4, 16 * CAP, MAXB, VB), F32),
            pltpu.VMEM((16 * CAP * 4, 8 * MAXB, VB), F32),
        ],
        compiler_params=pltpu.CompilerParams(vmem_limit_bytes=VMEM_LIMIT),
        cost_estimate=pl.CostEstimate(flops=4_000_000_000, bytes_accessed=8_000_000, transcendentals=0),
    )(units, total, limits, centres, own, other, coords)


def correct_kernel(limits, place, parts_ref, stations_ref, table_ref, out_ref):
    me, pol = place[0], place[1]
    row_side, col_side = pol // 2, pol % 2
    block = lax.broadcasted_iota(jnp.int32, (MAXB, VB), 0)

    def side(which):
        return [
            jnp.where(which == 1, table_ref[4:8, at : at + VB], table_ref[0:4, at : at + VB])
            for at in range(0, 4 * VB, VB)
        ]

    def entry(table, row, station):
        lane, chunk = station % VB, station // VB
        value = jnp.zeros((MAXB, VB), F32)
        for part in range(4):
            line = jnp.broadcast_to(table[part][row : row + 1], (MAXB, VB))
            value = jnp.where(chunk == part, jnp.take_along_axis(line, lane, axis=1), value)
        return value

    left_table, right_table = side(row_side), side(col_side)

    for c in range(CAP):
        left, right = stations_ref[c, 0], stations_ref[c, 1]
        lefts = [[entry(left_table, 2 * k + ri, left) for ri in range(2)] for k in range(2)]
        rights = [[entry(right_table, 2 * k + ri, right) for ri in range(2)] for k in range(2)]
        total_real = total_imag = jnp.zeros((MAXB, VB), F32)
        for inner_row in range(2):
            part_real = part_imag = jnp.zeros((MAXB, VB), F32)
            for inner_col in range(2):
                comp = parts_ref[0, 2 * inner_row + inner_col, c].astype(F32)
                for o in range(1, 16):
                    comp = comp + parts_ref[o, 2 * inner_row + inner_col, c].astype(F32)
                real, imag = comp[:MAXB], comp[MAXB:]
                right_real, right_imag = rights[inner_col]
                part_real = part_real + (real * right_real + imag * right_imag)
                part_imag = part_imag + (imag * right_real - real * right_imag)
            left_real, left_imag = lefts[inner_row]
            total_real = total_real + (left_real * part_real - left_imag * part_imag)
            total_imag = total_imag + (left_real * part_imag + left_imag * part_real)
        keep = block < limits[me * CAP + c]
        out_ref[0, 0, c] = jnp.where(keep, total_real, 0.0)
        out_ref[0, 1, c] = jnp.where(keep, total_imag, 0.0)


def correct(limits, place, parts, stations, table):
    smem = pl.BlockSpec(memory_space=pltpu.SMEM)
    vmem = pl.BlockSpec(memory_space=pltpu.VMEM)
    return pl.pallas_call(
        correct_kernel,
        out_shape=jax.ShapeDtypeStruct((1, 2, CAP, MAXB, VB), F32),
        in_specs=[smem] * 2 + [vmem] * 3,
        out_specs=vmem,
        compiler_params=pltpu.CompilerParams(vmem_limit_bytes=VMEM_LIMIT),
    )(limits, place, parts, stations, table)


def on_device(facets, owners, counts, coords, station_ids, jones_table):
    chip = lax.axis_index("z") * 4 + lax.axis_index("x")
    core = lax.axis_index("core")
    pol = lax.axis_index("pol")

    spread = jnp.broadcast_to(coords[None], (16,) + coords.shape)
    coords_all = lax.all_to_all(spread, ("z", "x"), split_axis=0, concat_axis=0, tiled=True)

    index = jnp.arange(S, dtype=jnp.int32)
    before = index[None, :] < index[:, None]
    mine = owners % 2 == core
    pairs = jnp.where(mine, (counts + 1) // 2, 0)
    rank = jnp.sum(jnp.where(before & (owners[None, :] == owners[:, None]), 1, 0), axis=1)
    first_unit = jnp.sum(jnp.where(before, pairs[None, :], 0), axis=1)
    slot = (owners // 2) * CAP + rank
    unit_index = jnp.arange(UNITS, dtype=jnp.int32)[:, None]
    offset = unit_index - first_unit[None, :]
    words = (slot * S + index)[None, :] * 4 + offset
    units = jnp.sum(jnp.where((offset >= 0) & (offset < pairs[None, :]), words, 0), axis=1)
    total = jnp.sum(pairs).reshape(1)
    slots = jnp.arange(16 * CAP, dtype=jnp.int32)[:, None]
    limits = jnp.sum(jnp.where((slots == slot[None, :]) & mine[None, :], counts[None, :], 0), axis=1)

    first_facet = 2 * (chip * 2 + core)
    other_facet = 2 * (chip * 2 + 1 - core)
    half = SG // 2
    centres = jnp.stack(
        [
            W * (first_facet // R) + (W // 2 - 0.5 - half),
            W * (first_facet % R) + (W - 0.5 - half),
            W * (other_facet % R) + (W - 0.5 - half),
        ]
    ).astype(F32)

    own = transform(facets[0])
    other = lax.ppermute(own, "core", [(0, 1), (1, 0)])
    parts = degrid(units, total, limits, centres, own, other, coords_all)
    parts = parts.reshape(64, CAP, 2 * MAXB, VB)
    parts = lax.all_to_all(parts, ("z", "x", "pol"), split_axis=0, concat_axis=0, tiled=True)
    parts = parts.reshape(16, 4, CAP, 2 * MAXB, VB)
    stations = jnp.moveaxis(station_ids, 2, 1)
    place = jnp.stack([chip, pol]).astype(jnp.int32)
    return correct(limits, place, parts, stations, jones_table)


def solution(mesh):
    split = jax.sharding.Mesh(mesh.devices.reshape(4, 4, 2, 4), ("z", "x", "core", "pol"))
    fs = ("z", "x", "core")
    return jax.shard_map(
        on_device,
        mesh=split,
        in_specs=(P("pol", fs, None, None), P(), P(), P(None, fs, None, None), P(fs, None, None, None), P()),
        out_specs=P("pol", None, fs, None, None),
        check_vma=False,
    )
```

```python
import functools
import math

import jax
import jax.numpy as jnp
import numpy as np
from jax import lax
from jax.experimental import pallas as pl
from jax.experimental.pallas import tpu as pltpu
from jax.sharding import PartitionSpec as P

R = 8
W = 64
S = 64
MAXB = 8
VB = 128
FH = 4096
SG = 512
CAP = 4
UNITS = 256
GROUP = 16
TOGETHER = 8
VMEM_LIMIT = 48 * 1024 * 1024
F32 = jnp.float32
BF16 = jnp.bfloat16


def first_table():
    index = np.arange(W)
    angles = (index[:, None] * index[None, :] % W) * (2.0 * math.pi / W)
    waves = np.concatenate([np.cos(angles[: W // 2 + 1]), np.sin(angles[1 : W // 2])], axis=0)
    return np.kron(waves, np.eye(GROUP)).astype(BF16)


def second_table():
    k1 = np.arange(W)[:, None, None]
    k2 = np.arange(S)[None, :, None]
    n1 = np.arange(W)[None, None, :]
    angles = (n1 * (k1 + W * k2) % FH) * (2.0 * math.pi / FH)
    cos, sin = np.cos(angles), np.sin(angles)
    sign = np.where(k1 % (W // 2) == 0, 0.0, np.where(k1 < W // 2, 1.0, -1.0))
    upper = np.concatenate([cos, -sin * sign], axis=2)
    lower = np.concatenate([sin, cos * sign], axis=2)
    return np.concatenate([upper, lower], axis=1).astype(BF16)


def mirror_table():
    table = np.zeros((2 * W, 2 * W), np.float32)
    index = np.arange(W)
    table[W - 1 - index, index] = 1.0
    table[2 * W - 1 - index, W + index] = 1.0
    return table.astype(BF16)


SIN_TERMS = (3.14159264, -5.16771008, 2.55007752, -0.598291286, 0.0776576603)
COS_TERMS = (0.999999953, -4.93479283, 4.05841135, -1.33187657, 0.219689611)


def polynomial(terms, x):
    total = jnp.full_like(x, terms[-1])
    for term in terms[-2::-1]:
        total = total * x + term
    return total


def turns_to_phase(turns):
    part = turns - jnp.round(turns)
    square = part * part
    half_sin = part * polynomial(SIN_TERMS, square)
    half_cos = polynomial(COS_TERMS, square)
    twice = half_sin + half_sin
    return (1.0 - twice * half_sin, twice * half_cos)


def rotate(cos, sin, step_cos, step_sin):
    return (cos * step_cos - sin * step_sin, sin * step_cos + cos * step_sin)


def transform_kernel(facets_ref, first_ref, second_ref, mirror_ref, out_ref, mirrored, sections, mixed):
    mirror = mirror_ref[...]
    half = W // 2

    @pl.loop(0, W // GROUP)
    def _(h):
        at = pl.ds(pl.multiple_of(h * GROUP, GROUP), GROUP)
        mirrored[...] = jnp.dot(
            facets_ref[0, :, at, :].reshape(W * GROUP, 2 * W), mirror, preferred_element_type=F32
        ).astype(BF16)
        strips = jnp.concatenate([mirrored[...], facets_ref[1, :, at, :].reshape(W * GROUP, 2 * W)], axis=1)
        for piece in range(4):
            rows = slice(piece * 256, piece * 256 + 256)
            part = jnp.dot(first_ref[rows, :], strips, preferred_element_type=F32).astype(BF16)
            for f in range(2):
                block = part[:, 2 * W * f : 2 * W * (f + 1)].reshape(16, GROUP, 2 * W)
                sections[f, piece * 16 : piece * 16 + 16, at, :] = block

    low_lanes = lax.broadcasted_iota(jnp.int32, (S, 2 * W), 1) < W

    def window(k1, fold):
        section = jnp.concatenate(
            [
                jnp.concatenate([sections[f, fold], sections[f, jnp.minimum(half + fold, W - 1)]], axis=0)
                for f in range(2)
            ],
            axis=1,
        )
        return jnp.dot(second_ref[k1], section, preferred_element_type=F32)

    @pl.loop(0, half // 4)
    def _(step):
        for inner in range(4):
            index = step * 4 + inner
            above = window(half + index, half - index)
            below = window(half - 1 - index, half - 1 - index)
            for pick, grid in enumerate((above + below, above - below)):
                cos_0, cos_1 = grid[:S, : 2 * W], grid[:S, 2 * W :]
                sin_0, sin_1 = grid[S:, : 2 * W], grid[S:, 2 * W :]
                cos_sum, cos_gap = cos_1 + cos_0, cos_1 - cos_0
                sin_sum, sin_gap = sin_1 + sin_0, sin_1 - sin_0
                real = jnp.where(low_lanes, cos_sum, cos_gap) + pltpu.roll(
                    jnp.where(low_lanes, -sin_gap, sin_sum), W, 1
                )
                imag = pltpu.roll(jnp.where(low_lanes, -cos_gap, cos_sum), W, 1) - jnp.where(
                    low_lanes, sin_sum, sin_gap
                )
                mixed[2 * pick, index] = real
                mixed[2 * pick + 1, index] = imag

    @pl.loop(0, S // 8)
    def _(step):
        at = pl.ds(pl.multiple_of(step * 8, 8), 8)
        for kind in range(4):
            for i in range(0, half, 16):
                halves = [jnp.swapaxes(mixed[kind, i + j : i + j + 8, at, :], 0, 1) for j in (0, 8)]
                rows = slice(half * kind + i, half * kind + i + 16)
                out_ref[at, rows, :] = jnp.concatenate(halves, axis=1).astype(BF16)


def transform(strips):
    return pl.pallas_call(
        transform_kernel,
        out_shape=jax.ShapeDtypeStruct((S, 2 * W, 2 * W), BF16),
        in_specs=[pl.BlockSpec(memory_space=pltpu.VMEM)] * 4,
        out_specs=pl.BlockSpec(memory_space=pltpu.VMEM),
        scratch_shapes=[
            pltpu.VMEM((W * GROUP, 2 * W), BF16),
            pltpu.VMEM((2, W, W, 2 * W), BF16),
            pltpu.VMEM((4, W // 2, S, 2 * W), F32),
        ],
        compiler_params=pltpu.CompilerParams(vmem_limit_bytes=VMEM_LIMIT),
        cost_estimate=pl.CostEstimate(flops=12_000_000_000, bytes_accessed=8_000_000, transcendentals=0),
        name="transform",
    )(strips.reshape(2, W, W, 2 * W), jnp.asarray(first_table()), jnp.asarray(second_table()), jnp.asarray(mirror_table()))


def degrid_kernel(together, units, total, limits, centres, own_ref, other_ref, coords_ref, out_ref, steps, sums):
    @pl.loop(0, 16)
    def _(o):
        for c in range(CAP):
            for axis in range(2):
                cos, sin = turns_to_phase(coords_ref[o, axis, c] * (8.0 / SG))
                steps[2 * axis, o * CAP + c] = cos
                steps[2 * axis + 1, o * CAP + c] = sin

    cells = (lax.broadcasted_iota(jnp.int32, (8, VB), 0).astype(F32) + 0.5) * (1.0 / SG)

    def ladder(position, step_cos, step_sin, count):
        cos, sin = turns_to_phase(position * cells)
        both = [(cos, sin)]
        step_cos = jnp.broadcast_to(step_cos, (8, VB))
        step_sin = jnp.broadcast_to(step_sin, (8, VB))
        for _ in range(count - 1):
            cos, sin = rotate(cos, sin, step_cos, step_sin)
            both.append((cos, sin))
        return both

    def place(index):
        word = units[index]
        g = word // (4 * S)
        kept = jnp.where(index < total[0], g, 16 * CAP)
        return (g // CAP, g % CAP, g, kept, (word // 4) % S, 2 * (word % 4))

    def phases_of(o, c, g, kept, s, b):
        blocks = []
        for h in range(2):
            row = pl.ds(b + h, 1)
            along = ladder(coords_ref[o, 1, c, row, :], steps[2, g, row, :], steps[3, g, row, :], 8)
            blocks.append(jnp.concatenate([t[0] for t in along] + [t[1] for t in along], axis=0).astype(BF16))
        return jnp.concatenate(blocks, axis=1)

    def finish(grid, o, c, g, kept, s, b):
        for h in range(2):
            row = pl.ds(b + h, 1)
            lanes = slice(VB * h, VB * (h + 1))
            weights = ladder(coords_ref[o, 0, c, row, :], steps[0, g, row, :], steps[1, g, row, :], 4)
            for q in range(2):
                real = imag = None
                for i, (cos, sin) in enumerate(weights):
                    at = 128 * q + 8 * i
                    sum_real, sum_imag = grid[at : at + 8, lanes], grid[at + 32 : at + 40, lanes]
                    gap_real, gap_imag = grid[at + 64 : at + 72, lanes], grid[at + 96 : at + 104, lanes]
                    step_real = cos * sum_real + sin * gap_imag
                    step_imag = cos * sum_imag - sin * gap_real
                    real = step_real if real is None else real + step_real
                    imag = step_imag if imag is None else imag + step_imag
                at = pl.ds(pl.multiple_of(8 * (b + h), 8), 8)
                sums[4 * kept + 2 * q, at, :] = real
                sums[4 * kept + 2 * q + 1, at, :] = imag

    @pl.loop(0, (total[0] + together - 1) // together)
    def _(step):
        at = [place(step * together + j) for j in range(together)]
        phases = [phases_of(*a) for a in at]
        grids = []
        for a, p in zip(at, phases):
            both = jnp.concatenate([own_ref[a[4]], other_ref[a[4]]], axis=0)
            grids.append(jnp.dot(both, p, preferred_element_type=F32))
        for a, grid in zip(at, grids):
            finish(grid, *a)

    centre_x, centre_own, centre_other = centres[0], centres[1], centres[2]

    @pl.loop(0, 16 * CAP)
    def _(g):
        o, c = g // CAP, g % CAP

        @pl.when(limits[g] > 0)
        def _():
            x, y = coords_ref[o, 0, c], coords_ref[o, 1, c]
            real = imag = jnp.zeros((MAXB, VB), F32)
            for q, centre_y in enumerate((centre_own, centre_other)):
                total_real = sums[4 * g + 2 * q, pl.ds(0, MAXB, stride=8), :]
                total_imag = sums[4 * g + 2 * q + 1, pl.ds(0, MAXB, stride=8), :]
                for r in range(1, 8):
                    total_real = total_real + sums[4 * g + 2 * q, pl.ds(r, MAXB, stride=8), :]
                    total_imag = total_imag + sums[4 * g + 2 * q + 1, pl.ds(r, MAXB, stride=8), :]
                cos, sin = turns_to_phase((x * centre_x + y * centre_y) * (1.0 / SG))
                real = real + (cos * total_real + sin * total_imag)
                imag = imag + (cos * total_imag - sin * total_real)
            scale = 1.0 / (math.sqrt(FH) * SG)
            value = (jnp.concatenate([real, imag], axis=0) * scale).astype(BF16)
            for copy in range(4):
                out_ref[o, copy, c] = value


def degrid(units, total, limits, centres, own, other, coords, together=TOGETHER):
    smem = pl.BlockSpec(memory_space=pltpu.SMEM)
    vmem = pl.BlockSpec(memory_space=pltpu.VMEM)
    return pl.pallas_call(
        functools.partial(degrid_kernel, together),
        out_shape=jax.ShapeDtypeStruct((16, 4, CAP, 2 * MAXB, VB), BF16),
        in_specs=[smem] * 4 + [vmem] * 3,
        out_specs=vmem,
        scratch_shapes=[
            pltpu.VMEM((4, 16 * CAP, MAXB, VB), F32),
            pltpu.VMEM(((16 * CAP + 1) * 4, 8 * MAXB, VB), F32),
        ],
        compiler_params=pltpu.CompilerParams(vmem_limit_bytes=VMEM_LIMIT),
        cost_estimate=pl.CostEstimate(flops=12_000_000_000, bytes_accessed=8_000_000, transcendentals=0),
        name="degrid",
    )(units, total, limits, centres, own, other, coords)


def correct_kernel(limits, place, parts_ref, stations_ref, table_ref, out_ref):
    me, pol = place[0], place[1]
    row_side, col_side = pol // 2, pol % 2
    block = lax.broadcasted_iota(jnp.int32, (MAXB, VB), 0)

    def side(which):
        return [
            jnp.where(which == 1, table_ref[4:8, at : at + VB], table_ref[0:4, at : at + VB])
            for at in range(0, 4 * VB, VB)
        ]

    def entry(table, row, station):
        lane, chunk = station % VB, station // VB
        value = jnp.zeros((MAXB, VB), F32)
        for part in range(4):
            line = jnp.broadcast_to(table[part][row : row + 1], (MAXB, VB))
            value = jnp.where(chunk == part, jnp.take_along_axis(line, lane, axis=1), value)
        return value

    left_table, right_table = side(row_side), side(col_side)

    for c in range(CAP):
        left, right = stations_ref[c, 0], stations_ref[c, 1]
        lefts = [[entry(left_table, 2 * k + ri, left) for ri in range(2)] for k in range(2)]
        rights = [[entry(right_table, 2 * k + ri, right) for ri in range(2)] for k in range(2)]
        total_real = total_imag = jnp.zeros((MAXB, VB), F32)
        for inner_row in range(2):
            part_real = part_imag = jnp.zeros((MAXB, VB), F32)
            for inner_col in range(2):
                comp = parts_ref[0, 2 * inner_row + inner_col, c].astype(F32)
                for o in range(1, 16):
                    comp = comp + parts_ref[o, 2 * inner_row + inner_col, c].astype(F32)
                real, imag = comp[:MAXB], comp[MAXB:]
                right_real, right_imag = rights[inner_col]
                part_real = part_real + (real * right_real + imag * right_imag)
                part_imag = part_imag + (imag * right_real - real * right_imag)
            left_real, left_imag = lefts[inner_row]
            total_real = total_real + (left_real * part_real - left_imag * part_imag)
            total_imag = total_imag + (left_real * part_imag + left_imag * part_real)
        keep = block < limits[me * CAP + c]
        out_ref[0, 0, c] = jnp.where(keep, total_real, 0.0)
        out_ref[0, 1, c] = jnp.where(keep, total_imag, 0.0)


def correct(limits, place, parts, stations, table):
    smem = pl.BlockSpec(memory_space=pltpu.SMEM)
    vmem = pl.BlockSpec(memory_space=pltpu.VMEM)
    return pl.pallas_call(
        correct_kernel,
        out_shape=jax.ShapeDtypeStruct((1, 2, CAP, MAXB, VB), F32),
        in_specs=[smem] * 2 + [vmem] * 3,
        out_specs=vmem,
        compiler_params=pltpu.CompilerParams(vmem_limit_bytes=VMEM_LIMIT),
        name="correct",
    )(limits, place, parts, stations, table)


def on_device(facets, owners, counts, coords, station_ids, jones_table):
    chip = lax.axis_index("z") * 4 + lax.axis_index("x")
    core = lax.axis_index("core")
    pol = lax.axis_index("pol")

    spread = jnp.broadcast_to(coords[None], (16,) + coords.shape)
    coords_all = lax.all_to_all(spread, ("z", "x"), split_axis=0, concat_axis=0, tiled=True)

    index = jnp.arange(S, dtype=jnp.int32)
    before = index[None, :] < index[:, None]
    mine = owners % 2 == core
    pairs = jnp.where(mine, (counts + 1) // 2, 0)
    rank = jnp.sum(jnp.where(before & (owners[None, :] == owners[:, None]), 1, 0), axis=1)
    first_unit = jnp.sum(jnp.where(before, pairs[None, :], 0), axis=1)
    slot = (owners // 2) * CAP + rank
    unit_index = jnp.arange(UNITS, dtype=jnp.int32)[:, None]
    offset = unit_index - first_unit[None, :]
    words = (slot * S + index)[None, :] * 4 + offset
    units = jnp.sum(jnp.where((offset >= 0) & (offset < pairs[None, :]), words, 0), axis=1)
    total = jnp.sum(pairs).reshape(1)
    slots = jnp.arange(16 * CAP, dtype=jnp.int32)[:, None]
    limits = jnp.sum(jnp.where((slots == slot[None, :]) & mine[None, :], counts[None, :], 0), axis=1)

    first_facet = 2 * (chip * 2 + core)
    other_facet = 2 * (chip * 2 + 1 - core)
    half = SG // 2
    centres = jnp.stack(
        [
            W * (first_facet // R) + (W // 2 - 0.5 - half),
            W * (first_facet % R) + (W - 0.5 - half),
            W * (other_facet % R) + (W - 0.5 - half),
        ]
    ).astype(F32)

    own = transform(facets[0])
    sent, coords_all = lax.optimization_barrier((own, coords_all))
    other = lax.ppermute(sent, "core", [(0, 1), (1, 0)])
    parts = degrid(units, total, limits, centres, own, other, coords_all)
    parts = parts.reshape(64, CAP, 2 * MAXB, VB)
    parts = lax.all_to_all(parts, ("z", "x", "pol"), split_axis=0, concat_axis=0, tiled=True)
    parts = parts.reshape(16, 4, CAP, 2 * MAXB, VB)
    stations = jnp.moveaxis(station_ids, 2, 1)
    place = jnp.stack([chip, pol]).astype(jnp.int32)
    return correct(limits, place, parts, stations, jones_table)


def solution(mesh):
    split = jax.sharding.Mesh(mesh.devices.reshape(4, 4, 2, 4), ("z", "x", "core", "pol"))
    fs = ("z", "x", "core")
    return jax.shard_map(
        on_device,
        mesh=split,
        in_specs=(P("pol", fs, None, None), P(), P(), P(None, fs, None, None), P(fs, None, None, None), P()),
        out_specs=P("pol", None, fs, None, None),
        check_vma=False,
    )
```

```python
import functools
import math

import jax
import jax.numpy as jnp
import numpy as np
from jax import lax
from jax.experimental import pallas as pl
from jax.experimental.pallas import tpu as pltpu
from jax.sharding import PartitionSpec as P

R = 8
W = 64
S = 64
MAXB = 8
VB = 128
FH = 4096
SG = 512
CAP = 4
UNITS = 256
GROUP = 16
TOGETHER = 8
VMEM_LIMIT = 48 * 1024 * 1024
F32 = jnp.float32
BF16 = jnp.bfloat16


def first_table():
    index = np.arange(W)
    angles = (index[:, None] * index[None, :] % W) * (2.0 * math.pi / W)
    waves = np.concatenate([np.cos(angles[: W // 2 + 1]), np.sin(angles[1 : W // 2])], axis=0)
    return np.kron(waves, np.eye(GROUP)).astype(BF16)


def second_table():
    k1 = np.arange(W)[:, None, None]
    k2 = np.arange(S)[None, :, None]
    n1 = np.arange(W)[None, None, :]
    angles = (n1 * (k1 + W * k2) % FH) * (2.0 * math.pi / FH)
    cos, sin = np.cos(angles), np.sin(angles)
    sign = np.where(k1 % (W // 2) == 0, 0.0, np.where(k1 < W // 2, 1.0, -1.0))
    upper = np.concatenate([cos, -sin * sign], axis=2)
    lower = np.concatenate([sin, cos * sign], axis=2)
    return np.concatenate([upper, lower], axis=1).astype(BF16)


SIN_TERMS = (3.14159264, -5.16771008, 2.55007752, -0.598291286, 0.0776576603)
COS_TERMS = (0.999999953, -4.93479283, 4.05841135, -1.33187657, 0.219689611)


def polynomial(terms, x):
    total = jnp.full_like(x, terms[-1])
    for term in terms[-2::-1]:
        total = total * x + term
    return total


def turns_to_phase(turns):
    part = turns - jnp.round(turns)
    square = part * part
    half_sin = part * polynomial(SIN_TERMS, square)
    half_cos = polynomial(COS_TERMS, square)
    twice = half_sin + half_sin
    return (1.0 - twice * half_sin, twice * half_cos)


def rotate(cos, sin, step_cos, step_sin):
    return (cos * step_cos - sin * step_sin, sin * step_cos + cos * step_sin)


def transform_kernel(
    facets_hbm, first_hbm, second_hbm, out_ref, facets_ref, first_ref, second_ref, sections, mixed, sems
):
    half = W // 2
    first_copy = pltpu.make_async_copy(first_hbm, first_ref, sems.at[0])
    second_copy = pltpu.make_async_copy(second_hbm, second_ref, sems.at[1])
    strip_copies = [
        pltpu.make_async_copy(facets_hbm.at[:, :, pl.ds(GROUP * h, GROUP), :], facets_ref.at[h], sems.at[2 + h])
        for h in range(W // GROUP)
    ]
    strip_copies[0].start()
    first_copy.start()
    for copy in strip_copies[1:]:
        copy.start()
    second_copy.start()
    row = lax.broadcasted_iota(jnp.int32, (2 * W, 2 * W), 0)
    lane = lax.broadcasted_iota(jnp.int32, (2 * W, 2 * W), 1)
    mirror = jnp.where(row == jnp.where(lane < W, W - 1, 3 * W - 1) - lane, 1.0, 0.0).astype(BF16)
    for h in range(W // GROUP):
        at = slice(GROUP * h, GROUP * h + GROUP)
        strip_copies[h].wait()
        mirrored = jnp.dot(
            facets_ref[h, 0].reshape(W * GROUP, 2 * W), mirror, preferred_element_type=F32
        ).astype(BF16)
        strips = jnp.concatenate([mirrored, facets_ref[h, 1].reshape(W * GROUP, 2 * W)], axis=1)
        if h == 0:
            first_copy.wait()
        for piece in range(4):
            rows = slice(piece * 256, piece * 256 + 256)
            part = jnp.dot(first_ref[rows, :], strips, preferred_element_type=F32).astype(BF16)
            for f in range(2):
                block = part[:, 2 * W * f : 2 * W * (f + 1)].reshape(16, GROUP, 2 * W)
                sections[f, piece * 16 : piece * 16 + 16, at, :] = block
    second_copy.wait()

    low_lanes = lax.broadcasted_iota(jnp.int32, (S, 2 * W), 1) < W

    def window(k1, fold):
        section = jnp.concatenate(
            [
                jnp.concatenate([sections[f, fold], sections[f, jnp.minimum(half + fold, W - 1)]], axis=0)
                for f in range(2)
            ],
            axis=1,
        )
        return jnp.dot(second_ref[k1], section, preferred_element_type=F32)

    @pl.loop(0, half // 4)
    def _(step):
        for inner in range(4):
            index = step * 4 + inner
            above = window(half + index, half - index)
            below = window(half - 1 - index, half - 1 - index)
            for pick, grid in enumerate((above + below, above - below)):
                cos_0, cos_1 = grid[:S, : 2 * W], grid[:S, 2 * W :]
                sin_0, sin_1 = grid[S:, : 2 * W], grid[S:, 2 * W :]
                cos_sum, cos_gap = cos_1 + cos_0, cos_1 - cos_0
                sin_sum, sin_gap = sin_1 + sin_0, sin_1 - sin_0
                real = jnp.where(low_lanes, cos_sum, cos_gap) + pltpu.roll(
                    jnp.where(low_lanes, -sin_gap, sin_sum), W, 1
                )
                imag = pltpu.roll(jnp.where(low_lanes, -cos_gap, cos_sum), W, 1) - jnp.where(
                    low_lanes, sin_sum, sin_gap
                )
                mixed[2 * pick, index] = real
                mixed[2 * pick + 1, index] = imag

    @pl.loop(0, S // 8)
    def _(step):
        at = pl.ds(pl.multiple_of(step * 8, 8), 8)
        for kind in range(4):
            for i in range(0, half, 16):
                halves = [jnp.swapaxes(mixed[kind, i + j : i + j + 8, at, :], 0, 1) for j in (0, 8)]
                rows = slice(half * kind + i, half * kind + i + 16)
                out_ref[at, rows, :] = jnp.concatenate(halves, axis=1).astype(BF16)


def in_hbm(array):
    return pltpu.with_memory_space_constraint(array, pltpu.HBM)


def transform(strips):
    return pl.pallas_call(
        transform_kernel,
        out_shape=jax.ShapeDtypeStruct((S, 2 * W, 2 * W), BF16),
        in_specs=[pl.BlockSpec(memory_space=pltpu.HBM)] * 3,
        out_specs=pl.BlockSpec(memory_space=pltpu.VMEM),
        scratch_shapes=[
            pltpu.VMEM((W // GROUP, 2, W, GROUP, 2 * W), BF16),
            pltpu.VMEM((W * GROUP, W * GROUP), BF16),
            pltpu.VMEM((W, 2 * W, 2 * W), BF16),
            pltpu.VMEM((2, W, W, 2 * W), BF16),
            pltpu.VMEM((4, W // 2, S, 2 * W), F32),
            pltpu.SemaphoreType.DMA((2 + W // GROUP,)),
        ],
        compiler_params=pltpu.CompilerParams(vmem_limit_bytes=VMEM_LIMIT),
        cost_estimate=pl.CostEstimate(flops=12_000_000_000, bytes_accessed=8_000_000, transcendentals=0),
        name="transform",
    )(*(in_hbm(x) for x in (strips.reshape(2, W, W, 2 * W), jnp.asarray(first_table()), jnp.asarray(second_table()))))


def degrid_kernel(together, units, total, limits, centres, own_ref, other_hbm, coords_ref, out_ref, steps, sums, other_ref, sem):
    other_copy = pltpu.make_async_copy(other_hbm, other_ref, sem)
    other_copy.start()

    @pl.loop(0, 16)
    def _(o):
        for c in range(CAP):
            for axis in range(2):
                cos, sin = turns_to_phase(coords_ref[o, axis * CAP + c] * (8.0 / SG))
                steps[2 * axis, o * CAP + c] = cos
                steps[2 * axis + 1, o * CAP + c] = sin

    other_copy.wait()
    cells = (lax.broadcasted_iota(jnp.int32, (8, VB), 0).astype(F32) + 0.5) * (1.0 / SG)

    def ladder(position, step_cos, step_sin, count):
        cos, sin = turns_to_phase(position * cells)
        both = [(cos, sin)]
        step_cos = jnp.broadcast_to(step_cos, (8, VB))
        step_sin = jnp.broadcast_to(step_sin, (8, VB))
        for _ in range(count - 1):
            cos, sin = rotate(cos, sin, step_cos, step_sin)
            both.append((cos, sin))
        return both

    def place(index):
        word = units[index]
        g = word // (4 * S)
        kept = jnp.where(index < total[0], g, 16 * CAP)
        return (g // CAP, g % CAP, g, kept, (word // 4) % S, 2 * (word % 4))

    def phases_of(o, c, g, kept, s, b):
        blocks = []
        for h in range(2):
            row = pl.ds(b + h, 1)
            along = ladder(coords_ref[o, CAP + c, row, :], steps[2, g, row, :], steps[3, g, row, :], 8)
            blocks.append(jnp.concatenate([t[0] for t in along] + [t[1] for t in along], axis=0).astype(BF16))
        return jnp.concatenate(blocks, axis=1)

    def finish(grid, o, c, g, kept, s, b):
        for h in range(2):
            row = pl.ds(b + h, 1)
            lanes = slice(VB * h, VB * (h + 1))
            weights = ladder(coords_ref[o, c, row, :], steps[0, g, row, :], steps[1, g, row, :], 4)
            for q in range(2):
                real = imag = None
                for i, (cos, sin) in enumerate(weights):
                    at = 128 * q + 8 * i
                    sum_real, sum_imag = grid[at : at + 8, lanes], grid[at + 32 : at + 40, lanes]
                    gap_real, gap_imag = grid[at + 64 : at + 72, lanes], grid[at + 96 : at + 104, lanes]
                    step_real = cos * sum_real + sin * gap_imag
                    step_imag = cos * sum_imag - sin * gap_real
                    real = step_real if real is None else real + step_real
                    imag = step_imag if imag is None else imag + step_imag
                at = pl.ds(pl.multiple_of(8 * (b + h), 8), 8)
                sums[4 * kept + 2 * q, at, :] = real
                sums[4 * kept + 2 * q + 1, at, :] = imag

    @pl.loop(0, (total[0] + together - 1) // together)
    def _(step):
        at = [place(step * together + j) for j in range(together)]
        phases = [phases_of(*a) for a in at]
        grids = []
        for a, p in zip(at, phases):
            both = jnp.concatenate([own_ref[a[4]], other_ref[a[4]]], axis=0)
            grids.append(jnp.dot(both, p, preferred_element_type=F32))
        for a, grid in zip(at, grids):
            finish(grid, *a)

    centre_x, centre_own, centre_other = centres[0], centres[1], centres[2]

    @pl.loop(0, 16 * CAP)
    def _(g):
        o, c = g // CAP, g % CAP

        @pl.when(limits[g] > 0)
        def _():
            x, y = coords_ref[o, c], coords_ref[o, CAP + c]
            real = imag = jnp.zeros((MAXB, VB), F32)
            for q, centre_y in enumerate((centre_own, centre_other)):
                total_real = sums[4 * g + 2 * q, pl.ds(0, MAXB, stride=8), :]
                total_imag = sums[4 * g + 2 * q + 1, pl.ds(0, MAXB, stride=8), :]
                for r in range(1, 8):
                    total_real = total_real + sums[4 * g + 2 * q, pl.ds(r, MAXB, stride=8), :]
                    total_imag = total_imag + sums[4 * g + 2 * q + 1, pl.ds(r, MAXB, stride=8), :]
                cos, sin = turns_to_phase((x * centre_x + y * centre_y) * (1.0 / SG))
                real = real + (cos * total_real + sin * total_imag)
                imag = imag + (cos * total_imag - sin * total_real)
            scale = 1.0 / (math.sqrt(FH) * SG)
            value = (jnp.concatenate([real, imag], axis=0) * scale).astype(BF16)
            for copy in range(4):
                out_ref[o * 4 + copy, pl.ds(pl.multiple_of(2 * MAXB * c, 2 * MAXB), 2 * MAXB), :] = value


def degrid(units, total, limits, centres, own, other, coords, together=TOGETHER):
    smem = pl.BlockSpec(memory_space=pltpu.SMEM)
    vmem = pl.BlockSpec(memory_space=pltpu.VMEM)
    return pl.pallas_call(
        functools.partial(degrid_kernel, together),
        out_shape=jax.ShapeDtypeStruct((64, CAP * 2 * MAXB, VB), BF16),
        in_specs=[smem] * 4 + [vmem, pl.BlockSpec(memory_space=pltpu.HBM), vmem],
        out_specs=vmem,
        scratch_shapes=[
            pltpu.VMEM((4, 16 * CAP, MAXB, VB), F32),
            pltpu.VMEM(((16 * CAP + 1) * 4, 8 * MAXB, VB), F32),
            pltpu.VMEM((S, 2 * W, 2 * W), BF16),
            pltpu.SemaphoreType.DMA,
        ],
        compiler_params=pltpu.CompilerParams(vmem_limit_bytes=VMEM_LIMIT),
        cost_estimate=pl.CostEstimate(flops=12_000_000_000, bytes_accessed=8_000_000, transcendentals=0),
        name="degrid",
    )(units, total, limits, centres, own, other, coords)


def correct_kernel(limits, place, parts_ref, stations_ref, table_ref, out_ref):
    me, pol = place[0], place[1]
    row_side, col_side = pol // 2, pol % 2
    block = lax.broadcasted_iota(jnp.int32, (MAXB, VB), 0)

    def side(which):
        return [
            jnp.where(which == 1, table_ref[4:8, at : at + VB], table_ref[0:4, at : at + VB])
            for at in range(0, 4 * VB, VB)
        ]

    def entry(table, row, station):
        lane, chunk = station % VB, station // VB
        value = jnp.zeros((MAXB, VB), F32)
        for part in range(4):
            line = jnp.broadcast_to(table[part][row : row + 1], (MAXB, VB))
            value = jnp.where(chunk == part, jnp.take_along_axis(line, lane, axis=1), value)
        return value

    left_table, right_table = side(row_side), side(col_side)

    for c in range(CAP):
        left, right = stations_ref[c, 0], stations_ref[c, 1]
        lefts = [[entry(left_table, 2 * k + ri, left) for ri in range(2)] for k in range(2)]
        rights = [[entry(right_table, 2 * k + ri, right) for ri in range(2)] for k in range(2)]
        total_real = total_imag = jnp.zeros((MAXB, VB), F32)
        for inner_row in range(2):
            part_real = part_imag = jnp.zeros((MAXB, VB), F32)
            for inner_col in range(2):
                rows = slice(2 * MAXB * c, 2 * MAXB * (c + 1))
                comp = parts_ref[2 * inner_row + inner_col, rows, :].astype(F32)
                for o in range(1, 16):
                    comp = comp + parts_ref[4 * o + 2 * inner_row + inner_col, rows, :].astype(F32)
                real, imag = comp[:MAXB], comp[MAXB:]
                right_real, right_imag = rights[inner_col]
                part_real = part_real + (real * right_real + imag * right_imag)
                part_imag = part_imag + (imag * right_real - real * right_imag)
            left_real, left_imag = lefts[inner_row]
            total_real = total_real + (left_real * part_real - left_imag * part_imag)
            total_imag = total_imag + (left_real * part_imag + left_imag * part_real)
        keep = block < limits[me * CAP + c]
        out_ref[0, 0, c] = jnp.where(keep, total_real, 0.0)
        out_ref[0, 1, c] = jnp.where(keep, total_imag, 0.0)


def correct(limits, place, parts, stations, table):
    smem = pl.BlockSpec(memory_space=pltpu.SMEM)
    vmem = pl.BlockSpec(memory_space=pltpu.VMEM)
    return pl.pallas_call(
        correct_kernel,
        out_shape=jax.ShapeDtypeStruct((1, 2, CAP, MAXB, VB), F32),
        in_specs=[smem] * 2 + [vmem] * 3,
        out_specs=vmem,
        compiler_params=pltpu.CompilerParams(vmem_limit_bytes=VMEM_LIMIT),
        name="correct",
    )(limits, place, parts, stations, table)


def on_device(facets, owners, counts, coords, station_ids, jones_table):
    chip = lax.axis_index("z") * 4 + lax.axis_index("x")
    core = lax.axis_index("core")
    pol = lax.axis_index("pol")

    spread = jnp.broadcast_to(coords.reshape(1, 2 * CAP * MAXB, VB), (16, 2 * CAP * MAXB, VB))
    coords_all = lax.all_to_all(spread, ("z", "x"), split_axis=0, concat_axis=0, tiled=True)

    coords_all = coords_all.reshape(16, 2 * CAP, MAXB, VB)

    index = jnp.arange(S, dtype=jnp.int32)
    before = index[None, :] < index[:, None]
    mine = owners % 2 == core
    pairs = jnp.where(mine, (counts + 1) // 2, 0)
    rank = jnp.sum(jnp.where(before & (owners[None, :] == owners[:, None]), 1, 0), axis=1)
    first_unit = jnp.sum(jnp.where(before, pairs[None, :], 0), axis=1)
    slot = (owners // 2) * CAP + rank
    unit_index = jnp.arange(UNITS, dtype=jnp.int32)[:, None]
    offset = unit_index - first_unit[None, :]
    words = (slot * S + index)[None, :] * 4 + offset
    units = jnp.sum(jnp.where((offset >= 0) & (offset < pairs[None, :]), words, 0), axis=1)
    total = jnp.sum(pairs).reshape(1)
    slots = jnp.arange(16 * CAP, dtype=jnp.int32)[:, None]
    limits = jnp.sum(jnp.where((slots == slot[None, :]) & mine[None, :], counts[None, :], 0), axis=1)

    first_facet = 2 * (chip * 2 + core)
    other_facet = 2 * (chip * 2 + 1 - core)
    half = SG // 2
    centres = jnp.stack(
        [
            W * (first_facet // R) + (W // 2 - 0.5 - half),
            W * (first_facet % R) + (W - 0.5 - half),
            W * (other_facet % R) + (W - 0.5 - half),
        ]
    ).astype(F32)

    own = transform(facets[0])
    sent, coords_all = lax.optimization_barrier((own, coords_all))
    other = lax.ppermute(sent, "core", [(0, 1), (1, 0)])
    parts = degrid(units, total, limits, centres, own, other, coords_all)
    parts = lax.all_to_all(parts, ("z", "x", "pol"), split_axis=0, concat_axis=0, tiled=True)
    stations = jnp.moveaxis(station_ids, 2, 1)
    place = jnp.stack([chip, pol]).astype(jnp.int32)
    return correct(limits, place, parts, stations, jones_table)


def solution(mesh):
    split = jax.sharding.Mesh(mesh.devices.reshape(4, 4, 2, 4), ("z", "x", "core", "pol"))
    fs = ("z", "x", "core")
    return jax.shard_map(
        on_device,
        mesh=split,
        in_specs=(P("pol", fs, None, None), P(), P(), P(None, fs, None, None), P(fs, None, None, None), P()),
        out_specs=P("pol", None, fs, None, None),
        check_vma=False,
    )
```

```python
import functools
import math

import jax
import jax.numpy as jnp
import numpy as np
from jax import lax
from jax.experimental import pallas as pl
from jax.experimental.pallas import tpu as pltpu
from jax.sharding import PartitionSpec as P

R = 8
W = 64
S = 64
MAXB = 8
VB = 128
FH = 4096
SG = 512
CAP = 4
UNITS = 256
TOTAL_AT = UNITS + 64
GROUP = 16
TOGETHER = 8
VMEM_LIMIT = 48 * 1024 * 1024
F32 = jnp.float32
BF16 = jnp.bfloat16


def first_table():
    index = np.arange(W)
    angles = (index[:, None] * index[None, :] % W) * (2.0 * math.pi / W)
    waves = np.concatenate([np.cos(angles[: W // 2 + 1]), np.sin(angles[1 : W // 2])], axis=0)
    return np.kron(waves, np.eye(GROUP)).astype(BF16)


def second_table():
    k1 = np.arange(W)[:, None, None]
    k2 = np.arange(S)[None, :, None]
    n1 = np.arange(W)[None, None, :]
    angles = (n1 * (k1 + W * k2) % FH) * (2.0 * math.pi / FH)
    cos, sin = np.cos(angles), np.sin(angles)
    sign = np.where(k1 % (W // 2) == 0, 0.0, np.where(k1 < W // 2, 1.0, -1.0))
    upper = np.concatenate([cos, -sin * sign], axis=2)
    lower = np.concatenate([sin, cos * sign], axis=2)
    return np.concatenate([upper, lower], axis=1).astype(BF16)


SIN_TERMS = (3.14159264, -5.16771008, 2.55007752, -0.598291286, 0.0776576603)
COS_TERMS = (0.999999953, -4.93479283, 4.05841135, -1.33187657, 0.219689611)


def polynomial(terms, x):
    total = jnp.full_like(x, terms[-1])
    for term in terms[-2::-1]:
        total = total * x + term
    return total


def turns_to_phase(turns):
    part = turns - jnp.round(turns)
    square = part * part
    half_sin = part * polynomial(SIN_TERMS, square)
    half_cos = polynomial(COS_TERMS, square)
    twice = half_sin + half_sin
    return (1.0 - twice * half_sin, twice * half_cos)


def rotate(cos, sin, step_cos, step_sin):
    return (cos * step_cos - sin * step_sin, sin * step_cos + cos * step_sin)


def transform_kernel(
    facets_hbm, first_hbm, second_hbm, out_ref, facets_ref, first_ref, second_ref, sections, mixed, sems
):
    half = W // 2
    first_copy = pltpu.make_async_copy(first_hbm, first_ref, sems.at[0])
    second_copy = pltpu.make_async_copy(second_hbm, second_ref, sems.at[1])
    strip_copies = [
        pltpu.make_async_copy(facets_hbm.at[:, :, pl.ds(GROUP * h, GROUP), :], facets_ref.at[h], sems.at[2 + h])
        for h in range(W // GROUP)
    ]
    strip_copies[0].start()
    first_copy.start()
    for copy in strip_copies[1:]:
        copy.start()
    second_copy.start()
    row = lax.broadcasted_iota(jnp.int32, (2 * W, 2 * W), 0)
    lane = lax.broadcasted_iota(jnp.int32, (2 * W, 2 * W), 1)
    mirror = jnp.where(row == jnp.where(lane < W, W - 1, 3 * W - 1) - lane, 1.0, 0.0).astype(BF16)
    for h in range(W // GROUP):
        at = slice(GROUP * h, GROUP * h + GROUP)
        strip_copies[h].wait()
        mirrored = jnp.dot(
            facets_ref[h, 0].reshape(W * GROUP, 2 * W), mirror, preferred_element_type=F32
        ).astype(BF16)
        strips = jnp.concatenate([mirrored, facets_ref[h, 1].reshape(W * GROUP, 2 * W)], axis=1)
        if h == 0:
            first_copy.wait()
        for piece in range(4):
            rows = slice(piece * 256, piece * 256 + 256)
            part = jnp.dot(first_ref[rows, :], strips, preferred_element_type=F32).astype(BF16)
            for f in range(2):
                block = part[:, 2 * W * f : 2 * W * (f + 1)].reshape(16, GROUP, 2 * W)
                sections[f, piece * 16 : piece * 16 + 16, at, :] = block
    second_copy.wait()

    low_lanes = lax.broadcasted_iota(jnp.int32, (S, 2 * W), 1) < W

    def window(k1, fold):
        section = jnp.concatenate(
            [
                jnp.concatenate([sections[f, fold], sections[f, jnp.minimum(half + fold, W - 1)]], axis=0)
                for f in range(2)
            ],
            axis=1,
        )
        return jnp.dot(second_ref[k1], section, preferred_element_type=F32)

    @pl.loop(0, half // 4)
    def _(step):
        for inner in range(4):
            index = step * 4 + inner
            above = window(half + index, half - index)
            below = window(half - 1 - index, half - 1 - index)
            for pick, grid in enumerate((above + below, above - below)):
                cos_0, cos_1 = grid[:S, : 2 * W], grid[:S, 2 * W :]
                sin_0, sin_1 = grid[S:, : 2 * W], grid[S:, 2 * W :]
                cos_sum, cos_gap = cos_1 + cos_0, cos_1 - cos_0
                sin_sum, sin_gap = sin_1 + sin_0, sin_1 - sin_0
                real = jnp.where(low_lanes, cos_sum, cos_gap) + pltpu.roll(
                    jnp.where(low_lanes, -sin_gap, sin_sum), W, 1
                )
                imag = pltpu.roll(jnp.where(low_lanes, -cos_gap, cos_sum), W, 1) - jnp.where(
                    low_lanes, sin_sum, sin_gap
                )
                mixed[2 * pick, index] = real
                mixed[2 * pick + 1, index] = imag

    @pl.loop(0, S // 8)
    def _(step):
        at = pl.ds(pl.multiple_of(step * 8, 8), 8)
        for kind in range(4):
            for i in range(0, half, 16):
                halves = [jnp.swapaxes(mixed[kind, i + j : i + j + 8, at, :], 0, 1) for j in (0, 8)]
                rows = slice(half * kind + i, half * kind + i + 16)
                out_ref[at, rows, :] = jnp.concatenate(halves, axis=1).astype(BF16)


def spread_kernel(coords_ref, out_hbm, sems):
    copies = [pltpu.make_async_copy(coords_ref, out_hbm.at[o], sems.at[o]) for o in range(16)]
    for copy in copies:
        copy.start()
    for copy in copies:
        copy.wait()


def spread(coords):
    return pl.pallas_call(
        spread_kernel,
        out_shape=jax.ShapeDtypeStruct((16,) + coords.shape, F32),
        in_specs=[pl.BlockSpec(memory_space=pltpu.VMEM)],
        out_specs=pl.BlockSpec(memory_space=pltpu.HBM),
        scratch_shapes=[pltpu.SemaphoreType.DMA((16,))],
        name="spread",
    )(coords)


def in_hbm(array):
    return pltpu.with_memory_space_constraint(array, pltpu.HBM)


def transform(strips):
    return pl.pallas_call(
        transform_kernel,
        out_shape=jax.ShapeDtypeStruct((S, 2 * W, 2 * W), BF16),
        in_specs=[pl.BlockSpec(memory_space=pltpu.HBM)] * 3,
        out_specs=pl.BlockSpec(memory_space=pltpu.VMEM),
        scratch_shapes=[
            pltpu.VMEM((W // GROUP, 2, W, GROUP, 2 * W), BF16),
            pltpu.VMEM((W * GROUP, W * GROUP), BF16),
            pltpu.VMEM((W, 2 * W, 2 * W), BF16),
            pltpu.VMEM((2, W, W, 2 * W), BF16),
            pltpu.VMEM((4, W // 2, S, 2 * W), F32),
            pltpu.SemaphoreType.DMA((2 + W // GROUP,)),
        ],
        compiler_params=pltpu.CompilerParams(vmem_limit_bytes=VMEM_LIMIT),
        cost_estimate=pl.CostEstimate(flops=12_000_000_000, bytes_accessed=8_000_000, transcendentals=0),
        name="transform",
    )(*(in_hbm(x) for x in (strips.reshape(2, W, W, 2 * W), jnp.asarray(first_table()), jnp.asarray(second_table()))))


def degrid_kernel(together, plan, own_ref, other_hbm, coords_ref, out_ref, steps, sums, other_ref, sem):
    other_copy = pltpu.make_async_copy(other_hbm, other_ref, sem)
    other_copy.start()

    @pl.loop(0, 16)
    def _(o):
        cos, sin = turns_to_phase(coords_ref[o] * (8.0 / SG))
        slots = pl.ds(o * CAP, CAP)
        for axis in range(2):
            steps[2 * axis, slots] = cos[CAP * axis : CAP * axis + CAP]
            steps[2 * axis + 1, slots] = sin[CAP * axis : CAP * axis + CAP]

    other_copy.wait()
    cells = (lax.broadcasted_iota(jnp.int32, (8, VB), 0).astype(F32) + 0.5) * (1.0 / SG)

    def ladder(position, step_cos, step_sin, count):
        cos, sin = turns_to_phase(position * cells)
        both = [(cos, sin)]
        step_cos = jnp.broadcast_to(step_cos, (8, VB))
        step_sin = jnp.broadcast_to(step_sin, (8, VB))
        for _ in range(count - 1):
            cos, sin = rotate(cos, sin, step_cos, step_sin)
            both.append((cos, sin))
        return both

    def place(index):
        word = plan[index]
        g = word // (4 * S)
        kept = jnp.where(index < plan[TOTAL_AT], g, 16 * CAP)
        return (g // CAP, g % CAP, g, kept, (word // 4) % S, 2 * (word % 4))

    def phases_of(o, c, g, kept, s, b):
        blocks = []
        for h in range(2):
            row = pl.ds(b + h, 1)
            along = ladder(coords_ref[o, CAP + c, row, :], steps[2, g, row, :], steps[3, g, row, :], 8)
            blocks.append(jnp.concatenate([t[0] for t in along] + [t[1] for t in along], axis=0).astype(BF16))
        return jnp.concatenate(blocks, axis=1)

    def finish(grid, o, c, g, kept, s, b):
        for h in range(2):
            row = pl.ds(b + h, 1)
            lanes = slice(VB * h, VB * (h + 1))
            weights = ladder(coords_ref[o, c, row, :], steps[0, g, row, :], steps[1, g, row, :], 4)
            for q in range(2):
                real = imag = None
                for i, (cos, sin) in enumerate(weights):
                    at = 128 * q + 8 * i
                    sum_real, sum_imag = grid[at : at + 8, lanes], grid[at + 32 : at + 40, lanes]
                    gap_real, gap_imag = grid[at + 64 : at + 72, lanes], grid[at + 96 : at + 104, lanes]
                    step_real = cos * sum_real + sin * gap_imag
                    step_imag = cos * sum_imag - sin * gap_real
                    real = step_real if real is None else real + step_real
                    imag = step_imag if imag is None else imag + step_imag
                at = pl.ds(pl.multiple_of(8 * (b + h), 8), 8)
                sums[4 * kept + 2 * q, at, :] = real
                sums[4 * kept + 2 * q + 1, at, :] = imag

    @pl.loop(0, (plan[TOTAL_AT] + together - 1) // together)
    def _(step):
        at = [place(step * together + j) for j in range(together)]
        phases = [phases_of(*a) for a in at]
        grids = []
        for a, p in zip(at, phases):
            both = jnp.concatenate([own_ref[a[4]], other_ref[a[4]]], axis=0)
            grids.append(jnp.dot(both, p, preferred_element_type=F32))
        for a, grid in zip(at, grids):
            finish(grid, *a)

    first_facet, other_facet = plan[TOTAL_AT + 1], plan[TOTAL_AT + 2]
    centre_x = (W * (first_facet // R)).astype(F32) + (W // 2 - 0.5 - SG // 2)
    centre_own = (W * (first_facet % R)).astype(F32) + (W - 0.5 - SG // 2)
    centre_other = (W * (other_facet % R)).astype(F32) + (W - 0.5 - SG // 2)

    @pl.loop(0, 16 * CAP)
    def _(g):
        o, c = g // CAP, g % CAP

        @pl.when(plan[UNITS + g] > 0)
        def _():
            x, y = coords_ref[o, c], coords_ref[o, CAP + c]
            real = imag = jnp.zeros((MAXB, VB), F32)
            for q, centre_y in enumerate((centre_own, centre_other)):
                total_real = sums[4 * g + 2 * q, pl.ds(0, MAXB, stride=8), :]
                total_imag = sums[4 * g + 2 * q + 1, pl.ds(0, MAXB, stride=8), :]
                for r in range(1, 8):
                    total_real = total_real + sums[4 * g + 2 * q, pl.ds(r, MAXB, stride=8), :]
                    total_imag = total_imag + sums[4 * g + 2 * q + 1, pl.ds(r, MAXB, stride=8), :]
                cos, sin = turns_to_phase((x * centre_x + y * centre_y) * (1.0 / SG))
                real = real + (cos * total_real + sin * total_imag)
                imag = imag + (cos * total_imag - sin * total_real)
            scale = 1.0 / (math.sqrt(FH) * SG)
            value = (jnp.concatenate([real, imag], axis=0) * scale).astype(BF16)
            out_ref[o, pl.ds(pl.multiple_of(2 * MAXB * c, 2 * MAXB), 2 * MAXB), :] = value


def degrid(plan, own, other, coords, together=TOGETHER):
    smem = pl.BlockSpec(memory_space=pltpu.SMEM)
    vmem = pl.BlockSpec(memory_space=pltpu.VMEM)
    return pl.pallas_call(
        functools.partial(degrid_kernel, together),
        out_shape=jax.ShapeDtypeStruct((16, CAP * 2 * MAXB, VB), BF16),
        in_specs=[smem, vmem, pl.BlockSpec(memory_space=pltpu.HBM), vmem],
        out_specs=vmem,
        scratch_shapes=[
            pltpu.VMEM((4, 16 * CAP, MAXB, VB), F32),
            pltpu.VMEM(((16 * CAP + 1) * 4, 8 * MAXB, VB), F32),
            pltpu.VMEM((S, 2 * W, 2 * W), BF16),
            pltpu.SemaphoreType.DMA,
        ],
        compiler_params=pltpu.CompilerParams(vmem_limit_bytes=VMEM_LIMIT),
        cost_estimate=pl.CostEstimate(flops=12_000_000_000, bytes_accessed=8_000_000, transcendentals=0),
        name="degrid",
    )(plan, own, other, coords)


def jones_kernel(place, stations_ref, table_ref, out_ref):
    pol = place[0]
    row_side, col_side = pol // 2, pol % 2

    def side(which):
        return [
            jnp.where(which == 1, table_ref[4:8, at : at + VB], table_ref[0:4, at : at + VB])
            for at in range(0, 4 * VB, VB)
        ]

    def entry(table, row, station):
        lane, chunk = station % VB, station // VB
        value = jnp.zeros((MAXB, VB), F32)
        for part in range(4):
            line = jnp.broadcast_to(table[part][row : row + 1], (MAXB, VB))
            value = jnp.where(chunk == part, jnp.take_along_axis(line, lane, axis=1), value)
        return value

    left_table, right_table = side(row_side), side(col_side)
    for c in range(CAP):
        left, right = stations_ref[c, 0], stations_ref[c, 1]
        lefts = [[entry(left_table, 2 * k + ri, left) for ri in range(2)] for k in range(2)]
        rights = [[entry(right_table, 2 * k + ri, right) for ri in range(2)] for k in range(2)]
        for turn in range(4):
            comp = (pol + 4 - turn) % 4
            left_real, left_imag = (jnp.where(comp // 2 == 1, lefts[1][ri], lefts[0][ri]) for ri in range(2))
            right_real, right_imag = (jnp.where(comp % 2 == 1, rights[1][ri], rights[0][ri]) for ri in range(2))
            out_ref[turn, c, 0] = left_real * right_real + left_imag * right_imag
            out_ref[turn, c, 1] = left_imag * right_real - left_real * right_imag


def jones(place, stations, table):
    smem = pl.BlockSpec(memory_space=pltpu.SMEM)
    vmem = pl.BlockSpec(memory_space=pltpu.VMEM)
    return pl.pallas_call(
        jones_kernel,
        out_shape=jax.ShapeDtypeStruct((4, CAP, 2, MAXB, VB), F32),
        in_specs=[smem, vmem, vmem],
        out_specs=vmem,
        compiler_params=pltpu.CompilerParams(vmem_limit_bytes=VMEM_LIMIT),
        name="jones",
    )(place, stations, table)


def correct_kernel(limits, jones_ref, own_ref, one_ref, two_ref, three_ref, out_ref):
    block = lax.broadcasted_iota(jnp.int32, (MAXB, VB), 0)
    for c in range(CAP):
        total_real = total_imag = jnp.zeros((MAXB, VB), F32)
        for turn, ref in enumerate((own_ref, one_ref, two_ref, three_ref)):
            at = 2 * MAXB * c
            real, imag = ref[at : at + MAXB, :], ref[at + MAXB : at + 2 * MAXB, :]
            step_real, step_imag = jones_ref[turn, c, 0], jones_ref[turn, c, 1]
            total_real = total_real + (step_real * real - step_imag * imag)
            total_imag = total_imag + (step_real * imag + step_imag * real)
        keep = block < limits[c]
        out_ref[0, 0, c] = jnp.where(keep, total_real, 0.0)
        out_ref[0, 1, c] = jnp.where(keep, total_imag, 0.0)


def correct(limits, factors, parts):
    smem = pl.BlockSpec(memory_space=pltpu.SMEM)
    vmem = pl.BlockSpec(memory_space=pltpu.VMEM)
    return pl.pallas_call(
        correct_kernel,
        out_shape=jax.ShapeDtypeStruct((1, 2, CAP, MAXB, VB), F32),
        in_specs=[smem] + [vmem] * 5,
        out_specs=vmem,
        compiler_params=pltpu.CompilerParams(vmem_limit_bytes=VMEM_LIMIT),
        name="correct",
    )(limits, factors, *parts)


def on_device(facets, owners, counts, coords, station_ids, jones_table):
    chip = lax.axis_index("z") * 4 + lax.axis_index("x")
    core = lax.axis_index("core")
    pol = lax.axis_index("pol")

    coords_all = lax.all_to_all(spread(coords.reshape(2 * CAP * MAXB, VB)), ("z", "x"), split_axis=0, concat_axis=0, tiled=True)

    coords_all = coords_all.reshape(16, 2 * CAP, MAXB, VB)

    index = jnp.arange(S, dtype=jnp.int32)
    before = index[None, :] < index[:, None]
    mine = owners % 2 == core
    pairs = jnp.where(mine, (counts + 1) // 2, 0)
    rank = jnp.sum(jnp.where(before & (owners[None, :] == owners[:, None]), 1, 0), axis=1)
    first_unit = jnp.sum(jnp.where(before, pairs[None, :], 0), axis=1)
    slot = (owners // 2) * CAP + rank
    unit_index = jnp.arange(UNITS, dtype=jnp.int32)[:, None]
    offset = unit_index - first_unit[None, :]
    words = (slot * S + index)[None, :] * 4 + offset
    units = jnp.sum(jnp.where((offset >= 0) & (offset < pairs[None, :]), words, 0), axis=1)
    slots = jnp.arange(16 * CAP, dtype=jnp.int32)[:, None]
    limits = jnp.sum(jnp.where((slots == slot[None, :]) & mine[None, :], counts[None, :], 0), axis=1)
    facet = 2 * (chip * 2 + core)
    extra = jnp.stack([jnp.sum(pairs), facet, facet + 2 - 4 * core])
    plan = jnp.concatenate([units, limits, extra, jnp.zeros((61,), jnp.int32)])
    own_limits = jnp.sum(
        jnp.where((slot[None, :] == chip * CAP + jnp.arange(CAP)[:, None]) & mine[None, :], counts[None, :], 0), axis=1
    )

    own = transform(facets[0])
    sent, coords_all = lax.optimization_barrier((own, coords_all))
    other = lax.ppermute(sent, "core", [(0, 1), (1, 0)])
    parts = degrid(plan, own, other, coords_all)
    parts = lax.all_to_all(parts, ("z", "x"), split_axis=0, concat_axis=0, tiled=True)
    visible = jnp.sum(parts.astype(F32), axis=0)
    factors = jones(pol.reshape(1).astype(jnp.int32), jnp.moveaxis(station_ids, 2, 1), jones_table)
    turns = [lax.ppermute(visible, "pol", [(i, (i + k) % 4) for i in range(4)]) for k in (1, 2, 3)]
    return correct(own_limits, factors, [visible] + turns)


def solution(mesh):
    split = jax.sharding.Mesh(mesh.devices.reshape(4, 4, 2, 4), ("z", "x", "core", "pol"))
    fs = ("z", "x", "core")
    return jax.shard_map(
        on_device,
        mesh=split,
        in_specs=(P("pol", fs, None, None), P(), P(), P(None, fs, None, None), P(fs, None, None, None), P()),
        out_specs=P("pol", None, fs, None, None),
        check_vma=False,
    )
```

```python
import functools
import math

import jax
import jax.numpy as jnp
import numpy as np
from jax import lax
from jax.experimental import pallas as pl
from jax.experimental.pallas import tpu as pltpu
from jax.sharding import PartitionSpec as P

R = 8
W = 64
S = 64
MAXB = 8
VB = 128
FH = 4096
SG = 512
CAP = 4
UNITS = 256
TOTAL_AT = UNITS + 64
GROUP = 16
TOGETHER = 8
VMEM_LIMIT = 48 * 1024 * 1024
F32 = jnp.float32
BF16 = jnp.bfloat16


def first_table():
    index = np.arange(W)
    angles = (index[:, None] * index[None, :] % W) * (2.0 * math.pi / W)
    waves = np.concatenate([np.cos(angles[: W // 2 + 1]), np.sin(angles[1 : W // 2])], axis=0)
    return np.repeat(waves, GROUP, axis=1).astype(BF16)


def second_table():
    k1 = np.arange(W)[:, None, None]
    k2 = np.arange(S)[None, :, None]
    n1 = np.arange(W)[None, None, :]
    angles = (n1 * (k1 + W * k2) % FH) * (2.0 * math.pi / FH)
    cos, sin = np.cos(angles), np.sin(angles)
    sign = np.where(k1 % (W // 2) == 0, 0.0, np.where(k1 < W // 2, 1.0, -1.0))
    upper = np.concatenate([cos, -sin * sign], axis=2)
    lower = np.concatenate([sin, cos * sign], axis=2)
    return np.concatenate([upper, lower], axis=1).astype(BF16)


SIN_TERMS = (3.14159264, -5.16771008, 2.55007752, -0.598291286, 0.0776576603)
COS_TERMS = (0.999999953, -4.93479283, 4.05841135, -1.33187657, 0.219689611)


def polynomial(terms, x):
    total = jnp.full_like(x, terms[-1])
    for term in terms[-2::-1]:
        total = total * x + term
    return total


def turns_to_phase(turns):
    part = turns - jnp.round(turns)
    square = part * part
    half_sin = part * polynomial(SIN_TERMS, square)
    half_cos = polynomial(COS_TERMS, square)
    twice = half_sin + half_sin
    return (1.0 - twice * half_sin, twice * half_cos)


def rotate(cos, sin, step_cos, step_sin):
    return (cos * step_cos - sin * step_sin, sin * step_cos + cos * step_sin)


def transform_kernel(
    facets_hbm, waves_hbm, second_hbm, out_ref, facets_ref, waves_ref, second_ref, first_ref, sections, mixed, sems
):
    half = W // 2
    wide = W * GROUP
    waves_copy = pltpu.make_async_copy(waves_hbm, waves_ref, sems.at[4])
    quarters = [pl.ds(16 * i, 16) for i in range(4)]
    second_copies = [
        pltpu.make_async_copy(second_hbm.at[at], second_ref.at[at], sems.at[i]) for i, at in enumerate(quarters)
    ]
    strip_copies = [
        pltpu.make_async_copy(facets_hbm.at[f, at], facets_ref.at[f, at], sems.at[5 + 4 * f + i])
        for f in range(2)
        for i, at in enumerate(quarters)
    ]
    for copy in [waves_copy] + strip_copies + second_copies:
        copy.start()
    row = lax.broadcasted_iota(jnp.int32, (2 * W, 2 * W), 0)
    lane = lax.broadcasted_iota(jnp.int32, (2 * W, 2 * W), 1)
    mirror = jnp.where(row == jnp.where(lane < W, W - 1, 3 * W - 1) - lane, 1.0, 0.0).astype(BF16)

    pieces = [slice(piece * 256, piece * 256 + 256) for piece in range(4)]
    cell = lax.broadcasted_iota(jnp.int32, (256, wide), 0) & (GROUP - 1)
    same = cell == (lax.broadcasted_iota(jnp.int32, (256, wide), 1) & (GROUP - 1))
    wave = lax.broadcasted_iota(jnp.int32, (256, W), 1)
    line = lax.broadcasted_iota(jnp.int32, (256, W), 0) >> 4
    waves_copy.wait()
    for piece, rows in enumerate(pieces):
        pick = jnp.where(line + 16 * piece == wave, 1.0, 0.0).astype(BF16)
        spread_waves = jnp.dot(pick, waves_ref[...], preferred_element_type=F32)
        first_ref[rows, :] = jnp.where(same, spread_waves, 0.0).astype(BF16)

    for copy in strip_copies:
        copy.wait()
    for h in range(W // GROUP):
        at = slice(GROUP * h, GROUP * h + GROUP)
        strip = [facets_ref[f, :, at, :].reshape(wide, 2 * W) for f in range(2)]
        mirrored = jnp.dot(strip[0], mirror, preferred_element_type=F32).astype(BF16)
        strips = jnp.concatenate([mirrored, strip[1]], axis=1)
        for piece, rows in enumerate(pieces):
            part = jnp.dot(first_ref[rows, :], strips, preferred_element_type=F32).astype(BF16)
            for f in range(2):
                block = part[:, 2 * W * f : 2 * W * (f + 1)].reshape(16, GROUP, 2 * W)
                sections[f, piece * 16 : piece * 16 + 16, at, :] = block
    for copy in second_copies:
        copy.wait()

    low_lanes = lax.broadcasted_iota(jnp.int32, (S, 2 * W), 1) < W

    def window(k1, fold):
        section = jnp.concatenate(
            [
                jnp.concatenate([sections[f, fold], sections[f, jnp.minimum(half + fold, W - 1)]], axis=0)
                for f in range(2)
            ],
            axis=1,
        )
        return jnp.dot(second_ref[k1], section, preferred_element_type=F32)

    @pl.loop(0, half // 16)
    def _(step):
        for inner in range(16):
            index = step * 16 + inner
            above = window(half + index, half - index)
            below = window(half - 1 - index, half - 1 - index)
            for pick, grid in enumerate((above + below, above - below)):
                cos_0, cos_1 = grid[:S, : 2 * W], grid[:S, 2 * W :]
                sin_0, sin_1 = grid[S:, : 2 * W], grid[S:, 2 * W :]
                cos_sum, cos_gap = cos_1 + cos_0, cos_1 - cos_0
                sin_sum, sin_gap = sin_1 + sin_0, sin_1 - sin_0
                real = jnp.where(low_lanes, cos_sum, cos_gap) + pltpu.roll(
                    jnp.where(low_lanes, -sin_gap, sin_sum), W, 1
                )
                imag = pltpu.roll(jnp.where(low_lanes, -cos_gap, cos_sum), W, 1) - jnp.where(
                    low_lanes, sin_sum, sin_gap
                )
                mixed[2 * pick, index] = real
                mixed[2 * pick + 1, index] = imag

    @pl.loop(0, S // 8)
    def _(step):
        at = pl.ds(pl.multiple_of(step * 8, 8), 8)
        for kind in range(4):
            for i in range(0, half, 16):
                halves = [jnp.swapaxes(mixed[kind, i + j : i + j + 8, at, :], 0, 1) for j in (0, 8)]
                rows = slice(half * kind + i, half * kind + i + 16)
                out_ref[at, rows, :] = jnp.concatenate(halves, axis=1).astype(BF16)


def spread_kernel(coords_ref, out_hbm, sems):
    copies = [pltpu.make_async_copy(coords_ref, out_hbm.at[o], sems.at[o]) for o in range(16)]
    for copy in copies:
        copy.start()
    for copy in copies:
        copy.wait()


def spread(coords):
    return pl.pallas_call(
        spread_kernel,
        out_shape=jax.ShapeDtypeStruct((16,) + coords.shape, F32),
        in_specs=[pl.BlockSpec(memory_space=pltpu.HBM)],
        out_specs=pl.BlockSpec(memory_space=pltpu.HBM),
        scratch_shapes=[pltpu.SemaphoreType.DMA((16,))],
        name="spread",
    )(in_hbm(coords))


def in_hbm(array):
    return pltpu.with_memory_space_constraint(array, pltpu.HBM)


def transform(strips):
    return pl.pallas_call(
        transform_kernel,
        out_shape=jax.ShapeDtypeStruct((S, 2 * W, 2 * W), BF16),
        in_specs=[pl.BlockSpec(memory_space=pltpu.HBM)] * 3,
        out_specs=pl.BlockSpec(memory_space=pltpu.VMEM),
        scratch_shapes=[
            pltpu.VMEM((2, W, W, 2 * W), BF16),
            pltpu.VMEM((W, W * GROUP), BF16),
            pltpu.VMEM((W, 2 * W, 2 * W), BF16),
            pltpu.VMEM((W * GROUP, W * GROUP), BF16),
            pltpu.VMEM((2, W, W, 2 * W), BF16),
            pltpu.VMEM((4, W // 2, S, 2 * W), F32),
            pltpu.SemaphoreType.DMA((13,)),
        ],
        compiler_params=pltpu.CompilerParams(vmem_limit_bytes=VMEM_LIMIT),
        cost_estimate=pl.CostEstimate(flops=12_000_000_000, bytes_accessed=8_000_000, transcendentals=0),
        name="transform",
    )(*(in_hbm(x) for x in (strips.reshape(2, W, W, 2 * W), jnp.asarray(first_table()), jnp.asarray(second_table()))))


def degrid_kernel(together, plan, own_ref, other_hbm, coords_ref, out_ref, steps, sums, other_ref, sem):
    other_copy = pltpu.make_async_copy(other_hbm, other_ref, sem)
    other_copy.start()

    @pl.loop(0, 16)
    def _(o):
        cos, sin = turns_to_phase(coords_ref[o] * (8.0 / SG))
        slots = pl.ds(o * CAP, CAP)
        for axis in range(2):
            steps[2 * axis, slots] = cos[CAP * axis : CAP * axis + CAP]
            steps[2 * axis + 1, slots] = sin[CAP * axis : CAP * axis + CAP]

    other_copy.wait()
    cells = (lax.broadcasted_iota(jnp.int32, (8, VB), 0).astype(F32) + 0.5) * (1.0 / SG)

    def ladder(position, step_cos, step_sin, count):
        cos, sin = turns_to_phase(position * cells)
        both = [(cos, sin)]
        step_cos = jnp.broadcast_to(step_cos, (8, VB))
        step_sin = jnp.broadcast_to(step_sin, (8, VB))
        for _ in range(count - 1):
            cos, sin = rotate(cos, sin, step_cos, step_sin)
            both.append((cos, sin))
        return both

    def place(index):
        word = plan[index]
        g = word >> 8
        kept = jnp.where(index < plan[TOTAL_AT], g, 16 * CAP)
        return (g >> 2, g & 3, g, kept, (word >> 2) & (S - 1), (word & 3) << 1)

    def phases_of(o, c, g, kept, s, b):
        blocks = []
        for h in range(2):
            row = pl.ds(b + h, 1)
            along = ladder(coords_ref[o, CAP + c, row, :], steps[2, g, row, :], steps[3, g, row, :], 8)
            blocks.append(jnp.concatenate([t[0] for t in along] + [t[1] for t in along], axis=0).astype(BF16))
        return jnp.concatenate(blocks, axis=1)

    def finish(grid, o, c, g, kept, s, b):
        for h in range(2):
            row = pl.ds(b + h, 1)
            lanes = slice(VB * h, VB * (h + 1))
            weights = ladder(coords_ref[o, c, row, :], steps[0, g, row, :], steps[1, g, row, :], 4)
            for q in range(2):
                real = imag = None
                for i, (cos, sin) in enumerate(weights):
                    at = 128 * q + 8 * i
                    sum_real, sum_imag = grid[at : at + 8, lanes], grid[at + 32 : at + 40, lanes]
                    gap_real, gap_imag = grid[at + 64 : at + 72, lanes], grid[at + 96 : at + 104, lanes]
                    step_real = cos * sum_real + sin * gap_imag
                    step_imag = cos * sum_imag - sin * gap_real
                    real = step_real if real is None else real + step_real
                    imag = step_imag if imag is None else imag + step_imag
                at = pl.ds(pl.multiple_of(8 * (b + h), 8), 8)
                sums[4 * kept + 2 * q, at, :] = real
                sums[4 * kept + 2 * q + 1, at, :] = imag

    @pl.loop(0, (plan[TOTAL_AT] + together - 1) // together)
    def _(step):
        at = [place(step * together + j) for j in range(together)]
        phases = [phases_of(*a) for a in at]
        grids = []
        for a, p in zip(at, phases):
            both = jnp.concatenate([own_ref[a[4]], other_ref[a[4]]], axis=0)
            grids.append(jnp.dot(both, p, preferred_element_type=F32))
        for a, grid in zip(at, grids):
            finish(grid, *a)

    first_facet, other_facet = plan[TOTAL_AT + 1], plan[TOTAL_AT + 2]
    centre_x = (W * (first_facet // R)).astype(F32) + (W // 2 - 0.5 - SG // 2)
    centre_own = (W * (first_facet % R)).astype(F32) + (W - 0.5 - SG // 2)
    centre_other = (W * (other_facet % R)).astype(F32) + (W - 0.5 - SG // 2)

    @pl.loop(0, 16)
    def _(o):
        for c in range(CAP):
            g = o * CAP + c
            x, y = coords_ref[o, c], coords_ref[o, CAP + c]
            real = imag = jnp.zeros((MAXB, VB), F32)
            for q, centre_y in enumerate((centre_own, centre_other)):
                total_real = sums[4 * g + 2 * q, pl.ds(0, MAXB, stride=8), :]
                total_imag = sums[4 * g + 2 * q + 1, pl.ds(0, MAXB, stride=8), :]
                for r in range(1, 8):
                    total_real = total_real + sums[4 * g + 2 * q, pl.ds(r, MAXB, stride=8), :]
                    total_imag = total_imag + sums[4 * g + 2 * q + 1, pl.ds(r, MAXB, stride=8), :]
                cos, sin = turns_to_phase((x * centre_x + y * centre_y) * (1.0 / SG))
                real = real + (cos * total_real + sin * total_imag)
                imag = imag + (cos * total_imag - sin * total_real)
            scale = 1.0 / (math.sqrt(FH) * SG)
            value = (jnp.concatenate([real, imag], axis=0) * scale).astype(BF16)
            out_ref[o, 2 * MAXB * c : 2 * MAXB * (c + 1), :] = value


def degrid(plan, own, other, coords, together=TOGETHER):
    smem = pl.BlockSpec(memory_space=pltpu.SMEM)
    vmem = pl.BlockSpec(memory_space=pltpu.VMEM)
    return pl.pallas_call(
        functools.partial(degrid_kernel, together),
        out_shape=jax.ShapeDtypeStruct((16, CAP * 2 * MAXB, VB), BF16),
        in_specs=[smem, vmem, pl.BlockSpec(memory_space=pltpu.HBM), vmem],
        out_specs=vmem,
        scratch_shapes=[
            pltpu.VMEM((4, 16 * CAP, MAXB, VB), F32),
            pltpu.VMEM(((16 * CAP + 1) * 4, 8 * MAXB, VB), F32),
            pltpu.VMEM((S, 2 * W, 2 * W), BF16),
            pltpu.SemaphoreType.DMA,
        ],
        compiler_params=pltpu.CompilerParams(vmem_limit_bytes=VMEM_LIMIT),
        cost_estimate=pl.CostEstimate(flops=12_000_000_000, bytes_accessed=8_000_000, transcendentals=0),
        name="degrid",
    )(plan, own, other, coords)


def jones_kernel(place, stations_ref, table_ref, out_ref, mask_ref):
    pol = place[0]
    row_side, col_side = pol // 2, pol % 2

    def side(which):
        return [
            jnp.where(which == 1, table_ref[4:8, at : at + VB], table_ref[0:4, at : at + VB])
            for at in range(0, 4 * VB, VB)
        ]

    def entry(table, row, station):
        lane, chunk = station % VB, station // VB
        value = jnp.zeros((MAXB, VB), F32)
        for part in range(4):
            line = jnp.broadcast_to(table[part][row : row + 1], (MAXB, VB))
            value = jnp.where(chunk == part, jnp.take_along_axis(line, lane, axis=1), value)
        return value

    left_table, right_table = side(row_side), side(col_side)
    block = lax.broadcasted_iota(jnp.int32, (MAXB, VB), 0)
    for c in range(CAP):
        mask_ref[c] = jnp.where(block < place[1 + c], 1.0, 0.0)
        left, right = stations_ref[c, 0], stations_ref[c, 1]
        lefts = [[entry(left_table, 2 * k + ri, left) for ri in range(2)] for k in range(2)]
        rights = [[entry(right_table, 2 * k + ri, right) for ri in range(2)] for k in range(2)]
        for turn in range(4):
            comp = (pol + 4 - turn) % 4
            left_real, left_imag = (jnp.where(comp // 2 == 1, lefts[1][ri], lefts[0][ri]) for ri in range(2))
            right_real, right_imag = (jnp.where(comp % 2 == 1, rights[1][ri], rights[0][ri]) for ri in range(2))
            out_ref[turn, c, 0] = left_real * right_real + left_imag * right_imag
            out_ref[turn, c, 1] = left_imag * right_real - left_real * right_imag


def jones(place, stations, table):
    smem = pl.BlockSpec(memory_space=pltpu.SMEM)
    vmem = pl.BlockSpec(memory_space=pltpu.VMEM)
    return pl.pallas_call(
        jones_kernel,
        out_shape=[
            jax.ShapeDtypeStruct((4, CAP, 2, MAXB, VB), F32),
            jax.ShapeDtypeStruct((CAP, MAXB, VB), F32),
        ],
        in_specs=[smem, vmem, vmem],
        out_specs=[vmem, vmem],
        compiler_params=pltpu.CompilerParams(vmem_limit_bytes=VMEM_LIMIT),
        name="jones",
    )(place, stations, table)


def correct_kernel(jones_ref, mask_ref, own_ref, one_ref, two_ref, three_ref, out_ref):
    for c in range(CAP):
        total_real = total_imag = jnp.zeros((MAXB, VB), F32)
        for turn, ref in enumerate((own_ref, one_ref, two_ref, three_ref)):
            at = 2 * MAXB * c
            real, imag = ref[at : at + MAXB, :], ref[at + MAXB : at + 2 * MAXB, :]
            step_real, step_imag = jones_ref[turn, c, 0], jones_ref[turn, c, 1]
            total_real = total_real + (step_real * real - step_imag * imag)
            total_imag = total_imag + (step_real * imag + step_imag * real)
        keep = mask_ref[c] > 0.0
        out_ref[0, 0, c] = jnp.where(keep, total_real, 0.0)
        out_ref[0, 1, c] = jnp.where(keep, total_imag, 0.0)


def correct(factors, mask, parts):
    vmem = pl.BlockSpec(memory_space=pltpu.VMEM)
    return pl.pallas_call(
        correct_kernel,
        out_shape=jax.ShapeDtypeStruct((1, 2, CAP, MAXB, VB), F32),
        in_specs=[vmem] * 6,
        out_specs=vmem,
        compiler_params=pltpu.CompilerParams(vmem_limit_bytes=VMEM_LIMIT),
        name="correct",
    )(factors, mask, *parts)


def on_device(facets, owners, counts, coords, station_ids, jones_table):
    chip = lax.axis_index("z") * 4 + lax.axis_index("x")
    core = lax.axis_index("core")
    pol = lax.axis_index("pol")

    coords_all = lax.all_to_all(spread(coords.reshape(2 * CAP * MAXB, VB)), ("z", "x"), split_axis=0, concat_axis=0, tiled=True)

    coords_all = coords_all.reshape(16, 2 * CAP, MAXB, VB)

    index = jnp.arange(S, dtype=jnp.int32)
    before = index[None, :] < index[:, None]
    mine = owners % 2 == core
    pairs = jnp.where(mine, (counts + 1) // 2, 0)
    rank = jnp.sum(jnp.where(before & (owners[None, :] == owners[:, None]), 1, 0), axis=1)
    first_unit = jnp.sum(jnp.where(before, pairs[None, :], 0), axis=1)
    slot = (owners // 2) * CAP + rank
    unit_index = jnp.arange(UNITS, dtype=jnp.int32)[:, None]
    offset = unit_index - first_unit[None, :]
    words = (slot * S + index)[None, :] * 4 + offset
    units = jnp.sum(jnp.where((offset >= 0) & (offset < pairs[None, :]), words, 0), axis=1)
    slots = jnp.arange(16 * CAP, dtype=jnp.int32)[:, None]
    limits = jnp.sum(jnp.where((slots == slot[None, :]) & mine[None, :], counts[None, :], 0), axis=1)
    facet = 2 * (chip * 2 + core)
    extra = jnp.stack([jnp.sum(pairs), facet, facet + 2 - 4 * core])
    plan = jnp.concatenate([units, limits, extra, jnp.zeros((61,), jnp.int32)])
    own_limits = jnp.sum(
        jnp.where((slot[None, :] == chip * CAP + jnp.arange(CAP)[:, None]) & mine[None, :], counts[None, :], 0), axis=1
    )

    own = transform(facets[0])
    sent, coords_all = lax.optimization_barrier((own, coords_all))
    other = lax.ppermute(sent, "core", [(0, 1), (1, 0)])
    parts = degrid(plan, own, other, coords_all)
    parts = lax.all_to_all(parts, ("z", "x"), split_axis=0, concat_axis=0, tiled=True)
    visible = jnp.sum(parts.astype(F32), axis=0)
    place = jnp.concatenate([pol.reshape(1), own_limits]).astype(jnp.int32)
    factors, mask = jones(place, jnp.moveaxis(station_ids, 2, 1), jones_table)
    turns = [lax.ppermute(visible, "pol", [(i, (i + k) % 4) for i in range(4)]) for k in (1, 2, 3)]
    return correct(factors, mask, [visible] + turns)


def solution(mesh):
    split = jax.sharding.Mesh(mesh.devices.reshape(4, 4, 2, 4), ("z", "x", "core", "pol"))
    fs = ("z", "x", "core")
    return jax.shard_map(
        on_device,
        mesh=split,
        in_specs=(P("pol", fs, None, None), P(), P(), P(None, fs, None, None), P(fs, None, None, None), P()),
        out_specs=P("pol", None, fs, None, None),
        check_vma=False,
    )
```

```python
import functools
import math

import jax
import jax.numpy as jnp
import numpy as np
from jax import lax
from jax.experimental import pallas as pl
from jax.experimental.pallas import tpu as pltpu
from jax.sharding import PartitionSpec as P

R = 8
W = 64
S = 64
MAXB = 8
VB = 128
FH = 4096
SG = 512
CAP = 4
UNITS = 256
TOTAL_AT = UNITS + 64
GROUP = 16
TOGETHER = 8
VMEM_LIMIT = 48 * 1024 * 1024
F32 = jnp.float32
BF16 = jnp.bfloat16


def first_table():
    index = np.arange(W)
    angles = (index[:, None] * index[None, :] % W) * (2.0 * math.pi / W)
    waves = np.concatenate([np.cos(angles[: W // 2 + 1]), np.sin(angles[1 : W // 2])], axis=0)
    return np.repeat(waves, GROUP, axis=1).astype(BF16)


def second_table():
    k1 = np.arange(W)[:, None, None]
    k2 = np.arange(S)[None, :, None]
    n1 = np.arange(W)[None, None, :]
    angles = (n1 * (k1 + W * k2) % FH) * (2.0 * math.pi / FH)
    cos, sin = np.cos(angles), np.sin(angles)
    sign = np.where(k1 % (W // 2) == 0, 0.0, np.where(k1 < W // 2, 1.0, -1.0))
    upper = np.concatenate([cos, -sin * sign], axis=2)
    lower = np.concatenate([sin, cos * sign], axis=2)
    return np.concatenate([upper, lower], axis=1).astype(BF16)


SIN_TERMS = (3.14159264, -5.16771008, 2.55007752, -0.598291286, 0.0776576603)
COS_TERMS = (0.999999953, -4.93479283, 4.05841135, -1.33187657, 0.219689611)


def polynomial(terms, x):
    total = jnp.full_like(x, terms[-1])
    for term in terms[-2::-1]:
        total = total * x + term
    return total


def turns_to_phase(turns):
    part = turns - jnp.round(turns)
    square = part * part
    half_sin = part * polynomial(SIN_TERMS, square)
    half_cos = polynomial(COS_TERMS, square)
    twice = half_sin + half_sin
    return (1.0 - twice * half_sin, twice * half_cos)


def rotate(cos, sin, step_cos, step_sin):
    return (cos * step_cos - sin * step_sin, sin * step_cos + cos * step_sin)


def transform_kernel(
    facets_hbm, waves_hbm, second_hbm, out_ref, facets_ref, waves_ref, second_ref, first_ref, sections, mixed, sems
):
    half = W // 2
    wide = W * GROUP
    waves_copy = pltpu.make_async_copy(waves_hbm, waves_ref, sems.at[4])
    quarters = [pl.ds(16 * i, 16) for i in range(4)]
    second_copies = [
        pltpu.make_async_copy(second_hbm.at[at], second_ref.at[at], sems.at[i]) for i, at in enumerate(quarters)
    ]
    strip_copies = [
        pltpu.make_async_copy(facets_hbm.at[f, at], facets_ref.at[f, at], sems.at[5 + 4 * f + i])
        for f in range(2)
        for i, at in enumerate(quarters)
    ]
    for copy in [waves_copy] + strip_copies + second_copies:
        copy.start()
    row = lax.broadcasted_iota(jnp.int32, (2 * W, 2 * W), 0)
    lane = lax.broadcasted_iota(jnp.int32, (2 * W, 2 * W), 1)
    mirror = jnp.where(row == jnp.where(lane < W, W - 1, 3 * W - 1) - lane, 1.0, 0.0).astype(BF16)

    pieces = [slice(piece * 256, piece * 256 + 256) for piece in range(4)]
    cell = lax.broadcasted_iota(jnp.int32, (256, wide), 0) & (GROUP - 1)
    same = cell == (lax.broadcasted_iota(jnp.int32, (256, wide), 1) & (GROUP - 1))
    wave = lax.broadcasted_iota(jnp.int32, (256, W), 1)
    line = lax.broadcasted_iota(jnp.int32, (256, W), 0) >> 4
    waves_copy.wait()
    for piece, rows in enumerate(pieces):
        pick = jnp.where(line + 16 * piece == wave, 1.0, 0.0).astype(BF16)
        spread_waves = jnp.dot(pick, waves_ref[...], preferred_element_type=F32)
        first_ref[rows, :] = jnp.where(same, spread_waves, 0.0).astype(BF16)

    for copy in strip_copies:
        copy.wait()
    for h in range(W // GROUP):
        at = slice(GROUP * h, GROUP * h + GROUP)
        strip = [facets_ref[f, :, at, :].reshape(wide, 2 * W) for f in range(2)]
        mirrored = jnp.dot(strip[0], mirror, preferred_element_type=F32).astype(BF16)
        strips = jnp.concatenate([mirrored, strip[1]], axis=1)
        for piece, rows in enumerate(pieces):
            part = jnp.dot(first_ref[rows, :], strips, preferred_element_type=F32).astype(BF16)
            for f in range(2):
                block = part[:, 2 * W * f : 2 * W * (f + 1)].reshape(16, GROUP, 2 * W)
                sections[f, piece * 16 : piece * 16 + 16, at, :] = block
    for copy in second_copies:
        copy.wait()

    low_lanes = lax.broadcasted_iota(jnp.int32, (S, 2 * W), 1) < W

    def window(k1, fold):
        section = jnp.concatenate(
            [
                jnp.concatenate([sections[f, fold], sections[f, jnp.minimum(half + fold, W - 1)]], axis=0)
                for f in range(2)
            ],
            axis=1,
        )
        return jnp.dot(second_ref[k1], section, preferred_element_type=F32)

    @pl.loop(0, half // 16)
    def _(step):
        for inner in range(16):
            index = step * 16 + inner
            above = window(half + index, half - index)
            below = window(half - 1 - index, half - 1 - index)
            for pick, grid in enumerate((above + below, above - below)):
                cos_0, cos_1 = grid[:S, : 2 * W], grid[:S, 2 * W :]
                sin_0, sin_1 = grid[S:, : 2 * W], grid[S:, 2 * W :]
                cos_sum, cos_gap = cos_1 + cos_0, cos_1 - cos_0
                sin_sum, sin_gap = sin_1 + sin_0, sin_1 - sin_0
                real = jnp.where(low_lanes, cos_sum, cos_gap) + pltpu.roll(
                    jnp.where(low_lanes, -sin_gap, sin_sum), W, 1
                )
                imag = pltpu.roll(jnp.where(low_lanes, -cos_gap, cos_sum), W, 1) - jnp.where(
                    low_lanes, sin_sum, sin_gap
                )
                mixed[2 * pick, index] = real
                mixed[2 * pick + 1, index] = imag

    @pl.loop(0, S // 8)
    def _(step):
        at = pl.ds(pl.multiple_of(step * 8, 8), 8)
        for kind in range(4):
            for i in range(0, half, 16):
                halves = [jnp.swapaxes(mixed[kind, i + j : i + j + 8, at, :], 0, 1) for j in (0, 8)]
                rows = slice(half * kind + i, half * kind + i + 16)
                out_ref[at, rows, :] = jnp.concatenate(halves, axis=1).astype(BF16)


def spread_kernel(coords_ref, out_hbm, sems):
    copies = [pltpu.make_async_copy(coords_ref, out_hbm.at[o], sems.at[o]) for o in range(16)]
    for copy in copies:
        copy.start()
    for copy in copies:
        copy.wait()


def spread(coords):
    return pl.pallas_call(
        spread_kernel,
        out_shape=jax.ShapeDtypeStruct((16,) + coords.shape, F32),
        in_specs=[pl.BlockSpec(memory_space=pltpu.VMEM)],
        out_specs=pl.BlockSpec(memory_space=pltpu.HBM),
        scratch_shapes=[pltpu.SemaphoreType.DMA((16,))],
        name="spread",
    )(coords)


def in_hbm(array):
    return pltpu.with_memory_space_constraint(array, pltpu.HBM)


def transform(strips):
    return pl.pallas_call(
        transform_kernel,
        out_shape=jax.ShapeDtypeStruct((S, 2 * W, 2 * W), BF16),
        in_specs=[pl.BlockSpec(memory_space=pltpu.HBM)] * 3,
        out_specs=pl.BlockSpec(memory_space=pltpu.VMEM),
        scratch_shapes=[
            pltpu.VMEM((2, W, W, 2 * W), BF16),
            pltpu.VMEM((W, W * GROUP), BF16),
            pltpu.VMEM((W, 2 * W, 2 * W), BF16),
            pltpu.VMEM((W * GROUP, W * GROUP), BF16),
            pltpu.VMEM((2, W, W, 2 * W), BF16),
            pltpu.VMEM((4, W // 2, S, 2 * W), F32),
            pltpu.SemaphoreType.DMA((13,)),
        ],
        compiler_params=pltpu.CompilerParams(vmem_limit_bytes=VMEM_LIMIT),
        cost_estimate=pl.CostEstimate(flops=12_000_000_000, bytes_accessed=8_000_000, transcendentals=0),
        name="transform",
    )(*(in_hbm(x) for x in (strips.reshape(2, W, W, 2 * W), jnp.asarray(first_table()), jnp.asarray(second_table()))))


def degrid_kernel(together, plan, own_ref, other_hbm, coords_ref, out_ref, steps, sums, other_ref, sem):
    other_copy = pltpu.make_async_copy(other_hbm, other_ref, sem)
    other_copy.start()

    @pl.loop(0, 16)
    def _(o):
        cos, sin = turns_to_phase(coords_ref[o] * (8.0 / SG))
        slots = pl.ds(o * CAP, CAP)
        for axis in range(2):
            steps[2 * axis, slots] = cos[CAP * axis : CAP * axis + CAP]
            steps[2 * axis + 1, slots] = sin[CAP * axis : CAP * axis + CAP]

    other_copy.wait()
    cells = (lax.broadcasted_iota(jnp.int32, (8, VB), 0).astype(F32) + 0.5) * (1.0 / SG)

    def ladder(position, step_cos, step_sin, count):
        cos, sin = turns_to_phase(position * cells)
        both = [(cos, sin)]
        step_cos = jnp.broadcast_to(step_cos, (8, VB))
        step_sin = jnp.broadcast_to(step_sin, (8, VB))
        for _ in range(count - 1):
            cos, sin = rotate(cos, sin, step_cos, step_sin)
            both.append((cos, sin))
        return both

    def place(index):
        word = plan[index]
        g = word >> 8
        kept = jnp.where(index < plan[TOTAL_AT], g, 16 * CAP)
        return (g >> 2, g & 3, g, kept, (word >> 2) & (S - 1), (word & 3) << 1)

    def phases_of(o, c, g, kept, s, b):
        blocks = []
        for h in range(2):
            row = pl.ds(b + h, 1)
            along = ladder(coords_ref[o, CAP + c, row, :], steps[2, g, row, :], steps[3, g, row, :], 8)
            blocks.append(jnp.concatenate([t[0] for t in along] + [t[1] for t in along], axis=0).astype(BF16))
        return jnp.concatenate(blocks, axis=1)

    def finish(grid, o, c, g, kept, s, b):
        for h in range(2):
            row = pl.ds(b + h, 1)
            lanes = slice(VB * h, VB * (h + 1))
            weights = ladder(coords_ref[o, c, row, :], steps[0, g, row, :], steps[1, g, row, :], 4)
            for q in range(2):
                real = imag = None
                for i, (cos, sin) in enumerate(weights):
                    at = 128 * q + 8 * i
                    sum_real, sum_imag = grid[at : at + 8, lanes], grid[at + 32 : at + 40, lanes]
                    gap_real, gap_imag = grid[at + 64 : at + 72, lanes], grid[at + 96 : at + 104, lanes]
                    step_real = cos * sum_real + sin * gap_imag
                    step_imag = cos * sum_imag - sin * gap_real
                    real = step_real if real is None else real + step_real
                    imag = step_imag if imag is None else imag + step_imag
                at = pl.ds(pl.multiple_of(8 * (b + h), 8), 8)
                sums[4 * kept + 2 * q, at, :] = real
                sums[4 * kept + 2 * q + 1, at, :] = imag

    @pl.loop(0, (plan[TOTAL_AT] + together - 1) // together)
    def _(step):
        at = [place(step * together + j) for j in range(together)]
        phases = [phases_of(*a) for a in at]
        grids = []
        for a, p in zip(at, phases):
            both = jnp.concatenate([own_ref[a[4]], other_ref[a[4]]], axis=0)
            grids.append(jnp.dot(both, p, preferred_element_type=F32))
        for a, grid in zip(at, grids):
            finish(grid, *a)

    first_facet, other_facet = plan[TOTAL_AT + 1], plan[TOTAL_AT + 2]
    centre_x = (W * (first_facet // R)).astype(F32) + (W // 2 - 0.5 - SG // 2)
    centre_own = (W * (first_facet % R)).astype(F32) + (W - 0.5 - SG // 2)
    centre_other = (W * (other_facet % R)).astype(F32) + (W - 0.5 - SG // 2)

    @pl.loop(0, 16)
    def _(o):
        for c in range(CAP):
            g = o * CAP + c
            x, y = coords_ref[o, c], coords_ref[o, CAP + c]
            real = imag = jnp.zeros((MAXB, VB), F32)
            for q, centre_y in enumerate((centre_own, centre_other)):
                total_real = sums[4 * g + 2 * q, pl.ds(0, MAXB, stride=8), :]
                total_imag = sums[4 * g + 2 * q + 1, pl.ds(0, MAXB, stride=8), :]
                for r in range(1, 8):
                    total_real = total_real + sums[4 * g + 2 * q, pl.ds(r, MAXB, stride=8), :]
                    total_imag = total_imag + sums[4 * g + 2 * q + 1, pl.ds(r, MAXB, stride=8), :]
                cos, sin = turns_to_phase((x * centre_x + y * centre_y) * (1.0 / SG))
                real = real + (cos * total_real + sin * total_imag)
                imag = imag + (cos * total_imag - sin * total_real)
            scale = 1.0 / (math.sqrt(FH) * SG)
            value = (jnp.concatenate([real, imag], axis=0) * scale).astype(BF16)
            out_ref[o, 2 * MAXB * c : 2 * MAXB * (c + 1), :] = value


def degrid(plan, own, other, coords, together=TOGETHER):
    smem = pl.BlockSpec(memory_space=pltpu.SMEM)
    vmem = pl.BlockSpec(memory_space=pltpu.VMEM)
    return pl.pallas_call(
        functools.partial(degrid_kernel, together),
        out_shape=jax.ShapeDtypeStruct((16, CAP * 2 * MAXB, VB), BF16),
        in_specs=[smem, vmem, pl.BlockSpec(memory_space=pltpu.HBM), vmem],
        out_specs=vmem,
        scratch_shapes=[
            pltpu.VMEM((4, 16 * CAP, MAXB, VB), F32),
            pltpu.VMEM(((16 * CAP + 1) * 4, 8 * MAXB, VB), F32),
            pltpu.VMEM((S, 2 * W, 2 * W), BF16),
            pltpu.SemaphoreType.DMA,
        ],
        compiler_params=pltpu.CompilerParams(vmem_limit_bytes=VMEM_LIMIT),
        cost_estimate=pl.CostEstimate(flops=12_000_000_000, bytes_accessed=8_000_000, transcendentals=0),
        name="degrid",
    )(plan, own, other, coords)


def jones_kernel(place, stations_ref, table_ref, out_ref, mask_ref):
    pol = place[0]
    row_side, col_side = pol // 2, pol % 2

    def side(which):
        return [
            jnp.where(which == 1, table_ref[4:8, at : at + VB], table_ref[0:4, at : at + VB])
            for at in range(0, 4 * VB, VB)
        ]

    def entry(table, row, station):
        lane, chunk = station % VB, station // VB
        value = jnp.zeros((MAXB, VB), F32)
        for part in range(4):
            line = jnp.broadcast_to(table[part][row : row + 1], (MAXB, VB))
            value = jnp.where(chunk == part, jnp.take_along_axis(line, lane, axis=1), value)
        return value

    left_table, right_table = side(row_side), side(col_side)
    block = lax.broadcasted_iota(jnp.int32, (MAXB, VB), 0)
    for c in range(CAP):
        mask_ref[c] = jnp.where(block < place[1 + c], 1.0, 0.0)
        left, right = stations_ref[c, 0], stations_ref[c, 1]
        lefts = [[entry(left_table, 2 * k + ri, left) for ri in range(2)] for k in range(2)]
        rights = [[entry(right_table, 2 * k + ri, right) for ri in range(2)] for k in range(2)]
        for turn in range(4):
            comp = (pol + 4 - turn) % 4
            left_real, left_imag = (jnp.where(comp // 2 == 1, lefts[1][ri], lefts[0][ri]) for ri in range(2))
            right_real, right_imag = (jnp.where(comp % 2 == 1, rights[1][ri], rights[0][ri]) for ri in range(2))
            out_ref[turn, c, 0] = left_real * right_real + left_imag * right_imag
            out_ref[turn, c, 1] = left_imag * right_real - left_real * right_imag


def jones(place, stations, table):
    smem = pl.BlockSpec(memory_space=pltpu.SMEM)
    vmem = pl.BlockSpec(memory_space=pltpu.VMEM)
    return pl.pallas_call(
        jones_kernel,
        out_shape=[
            jax.ShapeDtypeStruct((4, CAP, 2, MAXB, VB), F32),
            jax.ShapeDtypeStruct((CAP, MAXB, VB), F32),
        ],
        in_specs=[smem, vmem, vmem],
        out_specs=[vmem, vmem],
        compiler_params=pltpu.CompilerParams(vmem_limit_bytes=VMEM_LIMIT),
        name="jones",
    )(place, stations, table)


def correct_kernel(jones_ref, mask_ref, own_ref, one_ref, two_ref, three_ref, out_ref):
    for c in range(CAP):
        total_real = total_imag = jnp.zeros((MAXB, VB), F32)
        for turn, ref in enumerate((own_ref, one_ref, two_ref, three_ref)):
            at = 2 * MAXB * c
            real, imag = ref[at : at + MAXB, :], ref[at + MAXB : at + 2 * MAXB, :]
            step_real, step_imag = jones_ref[turn, c, 0], jones_ref[turn, c, 1]
            total_real = total_real + (step_real * real - step_imag * imag)
            total_imag = total_imag + (step_real * imag + step_imag * real)
        keep = mask_ref[c] > 0.0
        out_ref[0, 0, c] = jnp.where(keep, total_real, 0.0)
        out_ref[0, 1, c] = jnp.where(keep, total_imag, 0.0)


def correct(factors, mask, parts):
    vmem = pl.BlockSpec(memory_space=pltpu.VMEM)
    return pl.pallas_call(
        correct_kernel,
        out_shape=jax.ShapeDtypeStruct((1, 2, CAP, MAXB, VB), F32),
        in_specs=[vmem] * 6,
        out_specs=vmem,
        compiler_params=pltpu.CompilerParams(vmem_limit_bytes=VMEM_LIMIT),
        name="correct",
    )(factors, mask, *parts)


def on_device(facets, owners, counts, coords, station_ids, jones_table):
    chip = lax.axis_index("z") * 4 + lax.axis_index("x")
    core = lax.axis_index("core")
    pol = lax.axis_index("pol")

    coords_all = lax.all_to_all(spread(coords.reshape(2 * CAP * MAXB, VB)), ("z", "x"), split_axis=0, concat_axis=0, tiled=True)

    coords_all = coords_all.reshape(16, 2 * CAP, MAXB, VB)

    index = jnp.arange(S, dtype=jnp.int32)
    before = index[None, :] < index[:, None]
    mine = owners % 2 == core
    pairs = jnp.where(mine, (counts + 1) // 2, 0)
    rank = jnp.sum(jnp.where(before & (owners[None, :] == owners[:, None]), 1, 0), axis=1)
    first_unit = jnp.sum(jnp.where(before, pairs[None, :], 0), axis=1)
    slot = (owners // 2) * CAP + rank
    unit_index = jnp.arange(UNITS, dtype=jnp.int32)[:, None]
    offset = unit_index - first_unit[None, :]
    words = (slot * S + index)[None, :] * 4 + offset
    units = jnp.sum(jnp.where((offset >= 0) & (offset < pairs[None, :]), words, 0), axis=1)
    slots = jnp.arange(16 * CAP, dtype=jnp.int32)[:, None]
    limits = jnp.sum(jnp.where((slots == slot[None, :]) & mine[None, :], counts[None, :], 0), axis=1)
    facet = 2 * (chip * 2 + core)
    extra = jnp.stack([jnp.sum(pairs), facet, facet + 2 - 4 * core])
    plan = jnp.concatenate([units, limits, extra, jnp.zeros((61,), jnp.int32)])
    own_limits = jnp.sum(
        jnp.where((slot[None, :] == chip * CAP + jnp.arange(CAP)[:, None]) & mine[None, :], counts[None, :], 0), axis=1
    )

    own = transform(facets[0])
    sent, coords_all = lax.optimization_barrier((own, coords_all))
    other = lax.ppermute(sent, "core", [(0, 1), (1, 0)])
    parts = degrid(plan, own, other, coords_all)
    parts = lax.all_to_all(parts, ("z", "x"), split_axis=0, concat_axis=0, tiled=True)
    visible = jnp.sum(parts.astype(F32), axis=0)
    place = jnp.concatenate([pol.reshape(1), own_limits]).astype(jnp.int32)
    factors, mask = jones(place, jnp.moveaxis(station_ids, 2, 1), jones_table)
    turns = [lax.ppermute(visible, "pol", [(i, (i + k) % 4) for i in range(4)]) for k in (1, 2, 3)]
    return correct(factors, mask, [visible] + turns)


def solution(mesh):
    split = jax.sharding.Mesh(mesh.devices.reshape(4, 4, 2, 4), ("z", "x", "core", "pol"))
    fs = ("z", "x", "core")
    return jax.shard_map(
        on_device,
        mesh=split,
        in_specs=(P("pol", fs, None, None), P(), P(), P(None, fs, None, None), P(fs, None, None, None), P()),
        out_specs=P("pol", None, fs, None, None),
        check_vma=False,
    )
```

```python
import functools
import math

import jax
import jax.numpy as jnp
import numpy as np
from jax import lax
from jax.experimental import pallas as pl
from jax.experimental.pallas import tpu as pltpu
from jax.sharding import PartitionSpec as P

R = 8
W = 64
S = 64
MAXB = 8
VB = 128
FH = 4096
SG = 512
CAP = 4
UNITS = 256
TOTAL_AT = UNITS + 64
GROUP = 16
TOGETHER = 8
VMEM_LIMIT = 48 * 1024 * 1024
F32 = jnp.float32
BF16 = jnp.bfloat16


def first_table():
    index = np.arange(W)
    angles = (index[:, None] * index[None, :] % W) * (2.0 * math.pi / W)
    waves = np.concatenate([np.cos(angles[: W // 2 + 1]), np.sin(angles[1 : W // 2])], axis=0)
    return np.repeat(waves, GROUP, axis=1).astype(BF16)


def second_table():
    k1 = np.arange(W)[:, None, None]
    k2 = np.arange(S)[None, :, None]
    n1 = np.arange(W)[None, None, :]
    angles = (n1 * (k1 + W * k2) % FH) * (2.0 * math.pi / FH)
    cos, sin = np.cos(angles), np.sin(angles)
    sign = np.where(k1 % (W // 2) == 0, 0.0, np.where(k1 < W // 2, 1.0, -1.0))
    upper = np.concatenate([cos, -sin * sign], axis=2)
    lower = np.concatenate([sin, cos * sign], axis=2)
    return np.concatenate([upper, lower], axis=1).astype(BF16)


SIN_TERMS = (3.14159264, -5.16771008, 2.55007752, -0.598291286, 0.0776576603)
COS_TERMS = (0.999999953, -4.93479283, 4.05841135, -1.33187657, 0.219689611)


def polynomial(terms, x):
    total = jnp.full_like(x, terms[-1])
    for term in terms[-2::-1]:
        total = total * x + term
    return total


def turns_to_phase(turns):
    part = turns - jnp.round(turns)
    square = part * part
    half_sin = part * polynomial(SIN_TERMS, square)
    half_cos = polynomial(COS_TERMS, square)
    twice = half_sin + half_sin
    return (1.0 - twice * half_sin, twice * half_cos)


def rotate(cos, sin, step_cos, step_sin):
    return (cos * step_cos - sin * step_sin, sin * step_cos + cos * step_sin)


def transform_kernel(
    facets_hbm, waves_hbm, second_hbm, out_ref, facets_ref, waves_ref, second_ref, first_ref, sections, mixed, sems
):
    half = W // 2
    wide = W * GROUP
    waves_copy = pltpu.make_async_copy(waves_hbm, waves_ref, sems.at[4])
    quarters = [pl.ds(16 * i, 16) for i in range(4)]
    second_copies = [
        pltpu.make_async_copy(second_hbm.at[at], second_ref.at[at], sems.at[i]) for i, at in enumerate(quarters)
    ]
    strip_copies = [
        pltpu.make_async_copy(facets_hbm.at[f, at], facets_ref.at[f, at], sems.at[5 + 4 * f + i])
        for f in range(2)
        for i, at in enumerate(quarters)
    ]
    for copy in [waves_copy] + strip_copies + second_copies:
        copy.start()
    row = lax.broadcasted_iota(jnp.int32, (2 * W, 2 * W), 0)
    lane = lax.broadcasted_iota(jnp.int32, (2 * W, 2 * W), 1)
    mirror = jnp.where(row == jnp.where(lane < W, W - 1, 3 * W - 1) - lane, 1.0, 0.0).astype(BF16)

    pieces = [slice(piece * 256, piece * 256 + 256) for piece in range(4)]
    cell = lax.broadcasted_iota(jnp.int32, (256, wide), 0) & (GROUP - 1)
    same = cell == (lax.broadcasted_iota(jnp.int32, (256, wide), 1) & (GROUP - 1))
    wave = lax.broadcasted_iota(jnp.int32, (256, W), 1)
    line = lax.broadcasted_iota(jnp.int32, (256, W), 0) >> 4
    waves_copy.wait()
    for piece, rows in enumerate(pieces):
        pick = jnp.where(line + 16 * piece == wave, 1.0, 0.0).astype(BF16)
        spread_waves = jnp.dot(pick, waves_ref[...], preferred_element_type=F32)
        first_ref[rows, :] = jnp.where(same, spread_waves, 0.0).astype(BF16)

    for copy in strip_copies:
        copy.wait()
    for h in range(W // GROUP):
        at = slice(GROUP * h, GROUP * h + GROUP)
        strip = [facets_ref[f, :, at, :].reshape(wide, 2 * W) for f in range(2)]
        mirrored = jnp.dot(strip[0], mirror, preferred_element_type=F32).astype(BF16)
        strips = jnp.concatenate([mirrored, strip[1]], axis=1)
        for piece, rows in enumerate(pieces):
            part = jnp.dot(first_ref[rows, :], strips, preferred_element_type=F32).astype(BF16)
            for f in range(2):
                block = part[:, 2 * W * f : 2 * W * (f + 1)].reshape(16, GROUP, 2 * W)
                sections[f, piece * 16 : piece * 16 + 16, at, :] = block
    for copy in second_copies:
        copy.wait()

    low_lanes = lax.broadcasted_iota(jnp.int32, (S, 2 * W), 1) < W

    def window(k1, fold):
        section = jnp.concatenate(
            [
                jnp.concatenate([sections[f, fold], sections[f, jnp.minimum(half + fold, W - 1)]], axis=0)
                for f in range(2)
            ],
            axis=1,
        )
        return jnp.dot(second_ref[k1], section, preferred_element_type=F32)

    @pl.loop(0, half // 16)
    def _(step):
        for inner in range(16):
            index = step * 16 + inner
            above = window(half + index, half - index)
            below = window(half - 1 - index, half - 1 - index)
            for pick, grid in enumerate((above + below, above - below)):
                cos_0, cos_1 = grid[:S, : 2 * W], grid[:S, 2 * W :]
                sin_0, sin_1 = grid[S:, : 2 * W], grid[S:, 2 * W :]
                cos_sum, cos_gap = cos_1 + cos_0, cos_1 - cos_0
                sin_sum, sin_gap = sin_1 + sin_0, sin_1 - sin_0
                real = jnp.where(low_lanes, cos_sum, cos_gap) + pltpu.roll(
                    jnp.where(low_lanes, -sin_gap, sin_sum), W, 1
                )
                imag = pltpu.roll(jnp.where(low_lanes, -cos_gap, cos_sum), W, 1) - jnp.where(
                    low_lanes, sin_sum, sin_gap
                )
                mixed[2 * pick, index] = real
                mixed[2 * pick + 1, index] = imag

    @pl.loop(0, S // 8)
    def _(step):
        at = pl.ds(pl.multiple_of(step * 8, 8), 8)
        for kind in range(4):
            for i in range(0, half, 16):
                halves = [jnp.swapaxes(mixed[kind, i + j : i + j + 8, at, :], 0, 1) for j in (0, 8)]
                rows = slice(half * kind + i, half * kind + i + 16)
                out_ref[at, rows, :] = jnp.concatenate(halves, axis=1).astype(BF16)


def spread_kernel(coords_ref, out_hbm, sems):
    copies = [pltpu.make_async_copy(coords_ref, out_hbm.at[o], sems.at[o]) for o in range(16)]
    for copy in copies:
        copy.start()
    for copy in copies:
        copy.wait()


def spread(coords):
    return pl.pallas_call(
        spread_kernel,
        out_shape=jax.ShapeDtypeStruct((16,) + coords.shape, F32),
        in_specs=[pl.BlockSpec(memory_space=pltpu.VMEM)],
        out_specs=pl.BlockSpec(memory_space=pltpu.HBM),
        scratch_shapes=[pltpu.SemaphoreType.DMA((16,))],
        name="spread",
    )(coords)


def in_hbm(array):
    return pltpu.with_memory_space_constraint(array, pltpu.HBM)


def transform(strips):
    return pl.pallas_call(
        transform_kernel,
        out_shape=jax.ShapeDtypeStruct((S, 2 * W, 2 * W), BF16),
        in_specs=[pl.BlockSpec(memory_space=pltpu.HBM)] * 3,
        out_specs=pl.BlockSpec(memory_space=pltpu.VMEM),
        scratch_shapes=[
            pltpu.VMEM((2, W, W, 2 * W), BF16),
            pltpu.VMEM((W, W * GROUP), BF16),
            pltpu.VMEM((W, 2 * W, 2 * W), BF16),
            pltpu.VMEM((W * GROUP, W * GROUP), BF16),
            pltpu.VMEM((2, W, W, 2 * W), BF16),
            pltpu.VMEM((4, W // 2, S, 2 * W), F32),
            pltpu.SemaphoreType.DMA((13,)),
        ],
        compiler_params=pltpu.CompilerParams(vmem_limit_bytes=VMEM_LIMIT),
        cost_estimate=pl.CostEstimate(flops=12_000_000_000, bytes_accessed=8_000_000, transcendentals=0),
        name="transform",
    )(*(in_hbm(x) for x in (strips.reshape(2, W, W, 2 * W), jnp.asarray(first_table()), jnp.asarray(second_table()))))


def degrid_kernel(together, plan, own_ref, other_hbm, coords_ref, out_ref, steps, sums, other_ref, sem):
    other_copy = pltpu.make_async_copy(other_hbm, other_ref, sem)
    other_copy.start()

    rounds = (plan[TOTAL_AT + 3] + 3) >> 2

    @pl.loop(0, rounds)
    def _(step):
        for j in range(4):
            g = plan[UNITS + 4 * step + j]
            for axis in range(2):
                cos, sin = turns_to_phase(coords_ref[g >> 2, CAP * axis + (g & 3)] * (8.0 / SG))
                steps[2 * axis, g] = cos
                steps[2 * axis + 1, g] = sin

    other_copy.wait()
    cells = (lax.broadcasted_iota(jnp.int32, (8, VB), 0).astype(F32) + 0.5) * (1.0 / SG)

    def ladder(position, step_cos, step_sin, count):
        cos, sin = turns_to_phase(position * cells)
        both = [(cos, sin)]
        step_cos = jnp.broadcast_to(step_cos, (8, VB))
        step_sin = jnp.broadcast_to(step_sin, (8, VB))
        for _ in range(count - 1):
            cos, sin = rotate(cos, sin, step_cos, step_sin)
            both.append((cos, sin))
        return both

    def place(index):
        word = plan[index]
        g = word >> 8
        kept = jnp.where(index < plan[TOTAL_AT], g, 16 * CAP)
        return (g >> 2, g & 3, g, kept, (word >> 2) & (S - 1), (word & 3) << 1)

    def phases_of(o, c, g, kept, s, b):
        blocks = []
        for h in range(2):
            row = pl.ds(b + h, 1)
            along = ladder(coords_ref[o, CAP + c, row, :], steps[2, g, row, :], steps[3, g, row, :], 8)
            blocks.append(jnp.concatenate([t[0] for t in along] + [t[1] for t in along], axis=0).astype(BF16))
        return jnp.concatenate(blocks, axis=1)

    def finish(grid, o, c, g, kept, s, b):
        for h in range(2):
            row = pl.ds(b + h, 1)
            lanes = slice(VB * h, VB * (h + 1))
            weights = ladder(coords_ref[o, c, row, :], steps[0, g, row, :], steps[1, g, row, :], 4)
            for q in range(2):
                real = imag = None
                for i, (cos, sin) in enumerate(weights):
                    at = 128 * q + 8 * i
                    sum_real, sum_imag = grid[at : at + 8, lanes], grid[at + 32 : at + 40, lanes]
                    gap_real, gap_imag = grid[at + 64 : at + 72, lanes], grid[at + 96 : at + 104, lanes]
                    step_real = cos * sum_real + sin * gap_imag
                    step_imag = cos * sum_imag - sin * gap_real
                    real = step_real if real is None else real + step_real
                    imag = step_imag if imag is None else imag + step_imag
                at = pl.ds(pl.multiple_of(8 * (b + h), 8), 8)
                sums[4 * kept + 2 * q, at, :] = real
                sums[4 * kept + 2 * q + 1, at, :] = imag

    @pl.loop(0, (plan[TOTAL_AT] + together - 1) // together)
    def _(step):
        at = [place(step * together + j) for j in range(together)]
        phases = [phases_of(*a) for a in at]
        grids = []
        for a, p in zip(at, phases):
            both = jnp.concatenate([own_ref[a[4]], other_ref[a[4]]], axis=0)
            grids.append(jnp.dot(both, p, preferred_element_type=F32))
        for a, grid in zip(at, grids):
            finish(grid, *a)

    first_facet, other_facet = plan[TOTAL_AT + 1], plan[TOTAL_AT + 2]
    centre_x = (W * (first_facet // R)).astype(F32) + (W // 2 - 0.5 - SG // 2)
    centre_own = (W * (first_facet % R)).astype(F32) + (W - 0.5 - SG // 2)
    centre_other = (W * (other_facet % R)).astype(F32) + (W - 0.5 - SG // 2)

    @pl.loop(0, rounds)
    def _(step):
        for j in range(4):
            g = plan[UNITS + 4 * step + j]
            o, c = g >> 2, g & 3
            x, y = coords_ref[o, c], coords_ref[o, CAP + c]
            real = imag = jnp.zeros((MAXB, VB), F32)
            for q, centre_y in enumerate((centre_own, centre_other)):
                total_real = sums[4 * g + 2 * q, pl.ds(0, MAXB, stride=8), :]
                total_imag = sums[4 * g + 2 * q + 1, pl.ds(0, MAXB, stride=8), :]
                for r in range(1, 8):
                    total_real = total_real + sums[4 * g + 2 * q, pl.ds(r, MAXB, stride=8), :]
                    total_imag = total_imag + sums[4 * g + 2 * q + 1, pl.ds(r, MAXB, stride=8), :]
                cos, sin = turns_to_phase((x * centre_x + y * centre_y) * (1.0 / SG))
                real = real + (cos * total_real + sin * total_imag)
                imag = imag + (cos * total_imag - sin * total_real)
            scale = 1.0 / (math.sqrt(FH) * SG)
            value = (jnp.concatenate([real, imag], axis=0) * scale).astype(BF16)
            out_ref[o, pl.ds(pl.multiple_of(2 * MAXB * c, 2 * MAXB), 2 * MAXB), :] = value


def degrid(plan, own, other, coords, together=TOGETHER):
    smem = pl.BlockSpec(memory_space=pltpu.SMEM)
    vmem = pl.BlockSpec(memory_space=pltpu.VMEM)
    return pl.pallas_call(
        functools.partial(degrid_kernel, together),
        out_shape=jax.ShapeDtypeStruct((16, CAP * 2 * MAXB, VB), BF16),
        in_specs=[smem, vmem, pl.BlockSpec(memory_space=pltpu.HBM), vmem],
        out_specs=vmem,
        scratch_shapes=[
            pltpu.VMEM((4, 16 * CAP, MAXB, VB), F32),
            pltpu.VMEM(((16 * CAP + 1) * 4, 8 * MAXB, VB), F32),
            pltpu.VMEM((S, 2 * W, 2 * W), BF16),
            pltpu.SemaphoreType.DMA,
        ],
        compiler_params=pltpu.CompilerParams(vmem_limit_bytes=VMEM_LIMIT),
        cost_estimate=pl.CostEstimate(flops=12_000_000_000, bytes_accessed=8_000_000, transcendentals=0),
        name="degrid",
    )(plan, own, other, coords)


def jones_kernel(place, stations_ref, table_ref, out_ref, mask_ref):
    pol = place[0]
    row_side, col_side = pol // 2, pol % 2

    def side(which):
        return [
            jnp.where(which == 1, table_ref[4:8, at : at + VB], table_ref[0:4, at : at + VB])
            for at in range(0, 4 * VB, VB)
        ]

    def entry(table, row, station):
        lane, chunk = station % VB, station // VB
        value = jnp.zeros((MAXB, VB), F32)
        for part in range(4):
            line = jnp.broadcast_to(table[part][row : row + 1], (MAXB, VB))
            value = jnp.where(chunk == part, jnp.take_along_axis(line, lane, axis=1), value)
        return value

    left_table, right_table = side(row_side), side(col_side)
    block = lax.broadcasted_iota(jnp.int32, (MAXB, VB), 0)
    for c in range(CAP):
        mask_ref[c] = jnp.where(block < place[1 + c], 1.0, 0.0)
        left, right = stations_ref[c, 0], stations_ref[c, 1]
        lefts = [[entry(left_table, 2 * k + ri, left) for ri in range(2)] for k in range(2)]
        rights = [[entry(right_table, 2 * k + ri, right) for ri in range(2)] for k in range(2)]
        for turn in range(4):
            comp = (pol + 4 - turn) % 4
            left_real, left_imag = (jnp.where(comp // 2 == 1, lefts[1][ri], lefts[0][ri]) for ri in range(2))
            right_real, right_imag = (jnp.where(comp % 2 == 1, rights[1][ri], rights[0][ri]) for ri in range(2))
            out_ref[turn, c, 0] = left_real * right_real + left_imag * right_imag
            out_ref[turn, c, 1] = left_imag * right_real - left_real * right_imag


def jones(place, stations, table):
    smem = pl.BlockSpec(memory_space=pltpu.SMEM)
    vmem = pl.BlockSpec(memory_space=pltpu.VMEM)
    return pl.pallas_call(
        jones_kernel,
        out_shape=[
            jax.ShapeDtypeStruct((4, CAP, 2, MAXB, VB), F32),
            jax.ShapeDtypeStruct((CAP, MAXB, VB), F32),
        ],
        in_specs=[smem, vmem, vmem],
        out_specs=[vmem, vmem],
        compiler_params=pltpu.CompilerParams(vmem_limit_bytes=VMEM_LIMIT),
        name="jones",
    )(place, stations, table)


def correct_kernel(jones_ref, mask_ref, own_ref, one_ref, two_ref, three_ref, out_ref):
    for c in range(CAP):
        total_real = total_imag = jnp.zeros((MAXB, VB), F32)
        for turn, ref in enumerate((own_ref, one_ref, two_ref, three_ref)):
            at = 2 * MAXB * c
            real, imag = ref[at : at + MAXB, :], ref[at + MAXB : at + 2 * MAXB, :]
            step_real, step_imag = jones_ref[turn, c, 0], jones_ref[turn, c, 1]
            total_real = total_real + (step_real * real - step_imag * imag)
            total_imag = total_imag + (step_real * imag + step_imag * real)
        keep = mask_ref[c] > 0.0
        out_ref[0, 0, c] = jnp.where(keep, total_real, 0.0)
        out_ref[0, 1, c] = jnp.where(keep, total_imag, 0.0)


def correct(factors, mask, parts):
    vmem = pl.BlockSpec(memory_space=pltpu.VMEM)
    return pl.pallas_call(
        correct_kernel,
        out_shape=jax.ShapeDtypeStruct((1, 2, CAP, MAXB, VB), F32),
        in_specs=[vmem] * 6,
        out_specs=vmem,
        compiler_params=pltpu.CompilerParams(vmem_limit_bytes=VMEM_LIMIT),
        name="correct",
    )(factors, mask, *parts)


def on_device(facets, owners, counts, coords, station_ids, jones_table):
    chip = lax.axis_index("z") * 4 + lax.axis_index("x")
    core = lax.axis_index("core")
    pol = lax.axis_index("pol")

    coords_all = lax.all_to_all(spread(coords.reshape(2 * CAP * MAXB, VB)), ("z", "x"), split_axis=0, concat_axis=0, tiled=True)

    coords_all = coords_all.reshape(16, 2 * CAP, MAXB, VB)

    index = jnp.arange(S, dtype=jnp.int32)
    before = index[None, :] < index[:, None]
    mine = owners % 2 == core
    pairs = jnp.where(mine, (counts + 1) // 2, 0)
    rank = jnp.sum(jnp.where(before & (owners[None, :] == owners[:, None]), 1, 0), axis=1)
    first_unit = jnp.sum(jnp.where(before, pairs[None, :], 0), axis=1)
    slot = (owners // 2) * CAP + rank
    unit_index = jnp.arange(UNITS, dtype=jnp.int32)[:, None]
    offset = unit_index - first_unit[None, :]
    words = (slot * S + index)[None, :] * 4 + offset
    units = jnp.sum(jnp.where((offset >= 0) & (offset < pairs[None, :]), words, 0), axis=1)
    slots = jnp.arange(16 * CAP, dtype=jnp.int32)[:, None]
    place = jnp.sum(jnp.where(before & mine[None, :], 1, 0), axis=1)
    own_slots = jnp.sum(jnp.where((slots == place[None, :]) & mine[None, :], slot[None, :], 0), axis=1)
    facet = 2 * (chip * 2 + core)
    extra = jnp.stack([jnp.sum(pairs), facet, facet + 2 - 4 * core, jnp.sum(jnp.where(mine, 1, 0))])
    plan = jnp.concatenate([units, own_slots, extra, jnp.zeros((60,), jnp.int32)])
    own_limits = jnp.sum(
        jnp.where((slot[None, :] == chip * CAP + jnp.arange(CAP)[:, None]) & mine[None, :], counts[None, :], 0), axis=1
    )

    own = transform(facets[0])
    sent, coords_all = lax.optimization_barrier((own, coords_all))
    other = lax.ppermute(sent, "core", [(0, 1), (1, 0)])
    parts = degrid(plan, own, other, coords_all)
    parts = lax.all_to_all(parts, ("z", "x"), split_axis=0, concat_axis=0, tiled=True)
    visible = jnp.sum(parts.astype(F32), axis=0)
    place = jnp.concatenate([pol.reshape(1), own_limits]).astype(jnp.int32)
    factors, mask = jones(place, jnp.moveaxis(station_ids, 2, 1), jones_table)
    turns = [lax.ppermute(visible, "pol", [(i, (i + k) % 4) for i in range(4)]) for k in (1, 2, 3)]
    return correct(factors, mask, [visible] + turns)


def solution(mesh):
    split = jax.sharding.Mesh(mesh.devices.reshape(4, 4, 2, 4), ("z", "x", "core", "pol"))
    fs = ("z", "x", "core")
    return jax.shard_map(
        on_device,
        mesh=split,
        in_specs=(P("pol", fs, None, None), P(), P(), P(None, fs, None, None), P(fs, None, None, None), P()),
        out_specs=P("pol", None, fs, None, None),
        check_vma=False,
    )
```

```python
import functools
import math

import jax
import jax.numpy as jnp
import numpy as np
from jax import lax
from jax.experimental import pallas as pl
from jax.experimental.pallas import tpu as pltpu
from jax.sharding import PartitionSpec as P

R = 8
W = 64
S = 64
MAXB = 8
VB = 128
FH = 4096
SG = 512
CAP = 4
UNITS = 256
TOTAL_AT = UNITS + 64
GROUP = 16
TOGETHER = 8
VMEM_LIMIT = 48 * 1024 * 1024
F32 = jnp.float32
BF16 = jnp.bfloat16


def first_table():
    index = np.arange(W)
    angles = (index[:, None] * index[None, :] % W) * (2.0 * math.pi / W)
    waves = np.concatenate([np.cos(angles[: W // 2 + 1]), np.sin(angles[1 : W // 2])], axis=0)
    return np.repeat(waves, GROUP, axis=1).astype(BF16)


def second_table():
    k1 = np.arange(W)[:, None, None]
    k2 = np.arange(S)[None, :, None]
    n1 = np.arange(W)[None, None, :]
    angles = (n1 * (k1 + W * k2) % FH) * (2.0 * math.pi / FH)
    cos, sin = np.cos(angles), np.sin(angles)
    sign = np.where(k1 % (W // 2) == 0, 0.0, np.where(k1 < W // 2, 1.0, -1.0))
    upper = np.concatenate([cos, -sin * sign], axis=2)
    lower = np.concatenate([sin, cos * sign], axis=2)
    return np.concatenate([upper, lower], axis=1).astype(BF16)


SIN_TERMS = (3.14159264, -5.16771008, 2.55007752, -0.598291286, 0.0776576603)
COS_TERMS = (0.999999953, -4.93479283, 4.05841135, -1.33187657, 0.219689611)


def polynomial(terms, x):
    total = jnp.full_like(x, terms[-1])
    for term in terms[-2::-1]:
        total = total * x + term
    return total


def turns_to_phase(turns):
    part = turns - jnp.round(turns)
    square = part * part
    half_sin = part * polynomial(SIN_TERMS, square)
    half_cos = polynomial(COS_TERMS, square)
    twice = half_sin + half_sin
    return (1.0 - twice * half_sin, twice * half_cos)


def rotate(cos, sin, step_cos, step_sin):
    return (cos * step_cos - sin * step_sin, sin * step_cos + cos * step_sin)


def transform_kernel(
    facets_hbm, waves_hbm, second_hbm, coords_hbm, out_ref, spread_hbm,
    facets_ref, waves_ref, second_ref, coords_ref, first_ref, sections, mixed, sems, spread_sems,
):
    half = W // 2
    wide = W * GROUP
    waves_copy = pltpu.make_async_copy(waves_hbm, waves_ref, sems.at[4])
    quarters = [pl.ds(16 * i, 16) for i in range(4)]
    second_copies = [
        pltpu.make_async_copy(second_hbm.at[at], second_ref.at[at], sems.at[i]) for i, at in enumerate(quarters)
    ]
    strip_copies = [
        pltpu.make_async_copy(facets_hbm.at[f, at], facets_ref.at[f, at], sems.at[5 + 4 * f + i])
        for f in range(2)
        for i, at in enumerate(quarters)
    ]
    coords_copy = pltpu.make_async_copy(coords_hbm, coords_ref, sems.at[13])
    spread_copies = [pltpu.make_async_copy(coords_ref, spread_hbm.at[o], spread_sems.at[o]) for o in range(16)]
    for copy in [coords_copy, waves_copy] + strip_copies + second_copies:
        copy.start()
    row = lax.broadcasted_iota(jnp.int32, (2 * W, 2 * W), 0)
    lane = lax.broadcasted_iota(jnp.int32, (2 * W, 2 * W), 1)
    mirror = jnp.where(row == jnp.where(lane < W, W - 1, 3 * W - 1) - lane, 1.0, 0.0).astype(BF16)

    pieces = [slice(piece * 256, piece * 256 + 256) for piece in range(4)]
    cell = lax.broadcasted_iota(jnp.int32, (256, wide), 0) & (GROUP - 1)
    same = cell == (lax.broadcasted_iota(jnp.int32, (256, wide), 1) & (GROUP - 1))
    wave = lax.broadcasted_iota(jnp.int32, (256, W), 1)
    line = lax.broadcasted_iota(jnp.int32, (256, W), 0) >> 4
    waves_copy.wait()
    for piece, rows in enumerate(pieces):
        pick = jnp.where(line + 16 * piece == wave, 1.0, 0.0).astype(BF16)
        spread_waves = jnp.dot(pick, waves_ref[...], preferred_element_type=F32)
        first_ref[rows, :] = jnp.where(same, spread_waves, 0.0).astype(BF16)

    coords_copy.wait()
    for copy in spread_copies:
        copy.start()
    for copy in strip_copies:
        copy.wait()
    for h in range(W // GROUP):
        at = slice(GROUP * h, GROUP * h + GROUP)
        strip = [facets_ref[f, :, at, :].reshape(wide, 2 * W) for f in range(2)]
        mirrored = jnp.dot(strip[0], mirror, preferred_element_type=F32).astype(BF16)
        strips = jnp.concatenate([mirrored, strip[1]], axis=1)
        for piece, rows in enumerate(pieces):
            part = jnp.dot(first_ref[rows, :], strips, preferred_element_type=F32).astype(BF16)
            for f in range(2):
                block = part[:, 2 * W * f : 2 * W * (f + 1)].reshape(16, GROUP, 2 * W)
                sections[f, piece * 16 : piece * 16 + 16, at, :] = block
    for copy in second_copies:
        copy.wait()

    low_lanes = lax.broadcasted_iota(jnp.int32, (S, 2 * W), 1) < W

    def window(k1, fold):
        section = jnp.concatenate(
            [
                jnp.concatenate([sections[f, fold], sections[f, jnp.minimum(half + fold, W - 1)]], axis=0)
                for f in range(2)
            ],
            axis=1,
        )
        return jnp.dot(second_ref[k1], section, preferred_element_type=F32)

    @pl.loop(0, half // 16)
    def _(step):
        for inner in range(16):
            index = step * 16 + inner
            above = window(half + index, half - index)
            below = window(half - 1 - index, half - 1 - index)
            for pick, grid in enumerate((above + below, above - below)):
                cos_0, cos_1 = grid[:S, : 2 * W], grid[:S, 2 * W :]
                sin_0, sin_1 = grid[S:, : 2 * W], grid[S:, 2 * W :]
                cos_sum, cos_gap = cos_1 + cos_0, cos_1 - cos_0
                sin_sum, sin_gap = sin_1 + sin_0, sin_1 - sin_0
                real = jnp.where(low_lanes, cos_sum, cos_gap) + pltpu.roll(
                    jnp.where(low_lanes, -sin_gap, sin_sum), W, 1
                )
                imag = pltpu.roll(jnp.where(low_lanes, -cos_gap, cos_sum), W, 1) - jnp.where(
                    low_lanes, sin_sum, sin_gap
                )
                mixed[2 * pick, index] = real
                mixed[2 * pick + 1, index] = imag

    @pl.loop(0, S // 8)
    def _(step):
        at = pl.ds(pl.multiple_of(step * 8, 8), 8)
        for kind in range(4):
            for i in range(0, half, 16):
                halves = [jnp.swapaxes(mixed[kind, i + j : i + j + 8, at, :], 0, 1) for j in (0, 8)]
                rows = slice(half * kind + i, half * kind + i + 16)
                out_ref[at, rows, :] = jnp.concatenate(halves, axis=1).astype(BF16)

    for copy in spread_copies:
        copy.wait()


def in_hbm(array):
    return pltpu.with_memory_space_constraint(array, pltpu.HBM)


def transform(strips, coords):
    vmem = pl.BlockSpec(memory_space=pltpu.VMEM)
    hbm = pl.BlockSpec(memory_space=pltpu.HBM)
    return pl.pallas_call(
        transform_kernel,
        out_shape=[
            jax.ShapeDtypeStruct((S, 2 * W, 2 * W), BF16),
            jax.ShapeDtypeStruct((16,) + coords.shape, F32),
        ],
        in_specs=[hbm] * 4,
        out_specs=[vmem, hbm],
        scratch_shapes=[
            pltpu.VMEM((2, W, W, 2 * W), BF16),
            pltpu.VMEM((W, W * GROUP), BF16),
            pltpu.VMEM((W, 2 * W, 2 * W), BF16),
            pltpu.VMEM(coords.shape, F32),
            pltpu.VMEM((W * GROUP, W * GROUP), BF16),
            pltpu.VMEM((2, W, W, 2 * W), BF16),
            pltpu.VMEM((4, W // 2, S, 2 * W), F32),
            pltpu.SemaphoreType.DMA((14,)),
            pltpu.SemaphoreType.DMA((16,)),
        ],
        compiler_params=pltpu.CompilerParams(vmem_limit_bytes=VMEM_LIMIT),
        cost_estimate=pl.CostEstimate(flops=12_000_000_000, bytes_accessed=8_000_000, transcendentals=0),
        name="transform",
    )(*(in_hbm(x) for x in (strips.reshape(2, W, W, 2 * W), jnp.asarray(first_table()), jnp.asarray(second_table()), coords)))


def degrid_kernel(together, plan, own_ref, other_hbm, coords_ref, out_ref, steps, sums, other_ref, sem):
    other_copy = pltpu.make_async_copy(other_hbm, other_ref, sem)
    other_copy.start()

    rounds = (plan[TOTAL_AT + 3] + 3) >> 2

    @pl.loop(0, rounds)
    def _(step):
        for j in range(4):
            g = plan[UNITS + 4 * step + j]
            for axis in range(2):
                cos, sin = turns_to_phase(coords_ref[g >> 2, CAP * axis + (g & 3)] * (8.0 / SG))
                steps[2 * axis, g] = cos
                steps[2 * axis + 1, g] = sin

    other_copy.wait()
    cells = (lax.broadcasted_iota(jnp.int32, (8, VB), 0).astype(F32) + 0.5) * (1.0 / SG)

    def ladder(position, step_cos, step_sin, count):
        cos, sin = turns_to_phase(position * cells)
        both = [(cos, sin)]
        step_cos = jnp.broadcast_to(step_cos, (8, VB))
        step_sin = jnp.broadcast_to(step_sin, (8, VB))
        for _ in range(count - 1):
            cos, sin = rotate(cos, sin, step_cos, step_sin)
            both.append((cos, sin))
        return both

    def place(index):
        word = plan[index]
        g = word >> 8
        kept = jnp.where(index < plan[TOTAL_AT], g, 16 * CAP)
        return (g >> 2, g & 3, g, kept, (word >> 2) & (S - 1), (word & 3) << 1)

    def phases_of(o, c, g, kept, s, b):
        blocks = []
        for h in range(2):
            row = pl.ds(b + h, 1)
            along = ladder(coords_ref[o, CAP + c, row, :], steps[2, g, row, :], steps[3, g, row, :], 8)
            blocks.append(jnp.concatenate([t[0] for t in along] + [t[1] for t in along], axis=0).astype(BF16))
        return jnp.concatenate(blocks, axis=1)

    def finish(grid, o, c, g, kept, s, b):
        for h in range(2):
            row = pl.ds(b + h, 1)
            lanes = slice(VB * h, VB * (h + 1))
            weights = ladder(coords_ref[o, c, row, :], steps[0, g, row, :], steps[1, g, row, :], 4)
            for q in range(2):
                real = imag = None
                for i, (cos, sin) in enumerate(weights):
                    at = 128 * q + 8 * i
                    sum_real, sum_imag = grid[at : at + 8, lanes], grid[at + 32 : at + 40, lanes]
                    gap_real, gap_imag = grid[at + 64 : at + 72, lanes], grid[at + 96 : at + 104, lanes]
                    step_real = cos * sum_real + sin * gap_imag
                    step_imag = cos * sum_imag - sin * gap_real
                    real = step_real if real is None else real + step_real
                    imag = step_imag if imag is None else imag + step_imag
                at = pl.ds(pl.multiple_of(8 * (b + h), 8), 8)
                sums[4 * kept + 2 * q, at, :] = real
                sums[4 * kept + 2 * q + 1, at, :] = imag

    @pl.loop(0, (plan[TOTAL_AT] + together - 1) // together)
    def _(step):
        at = [place(step * together + j) for j in range(together)]
        phases = [phases_of(*a) for a in at]
        grids = []
        for a, p in zip(at, phases):
            both = jnp.concatenate([own_ref[a[4]], other_ref[a[4]]], axis=0)
            grids.append(jnp.dot(both, p, preferred_element_type=F32))
        for a, grid in zip(at, grids):
            finish(grid, *a)

    first_facet, other_facet = plan[TOTAL_AT + 1], plan[TOTAL_AT + 2]
    centre_x = (W * (first_facet // R)).astype(F32) + (W // 2 - 0.5 - SG // 2)
    centre_own = (W * (first_facet % R)).astype(F32) + (W - 0.5 - SG // 2)
    centre_other = (W * (other_facet % R)).astype(F32) + (W - 0.5 - SG // 2)

    @pl.loop(0, rounds)
    def _(step):
        for j in range(4):
            g = plan[UNITS + 4 * step + j]
            o, c = g >> 2, g & 3
            x, y = coords_ref[o, c], coords_ref[o, CAP + c]
            real = imag = jnp.zeros((MAXB, VB), F32)
            for q, centre_y in enumerate((centre_own, centre_other)):
                total_real = sums[4 * g + 2 * q, pl.ds(0, MAXB, stride=8), :]
                total_imag = sums[4 * g + 2 * q + 1, pl.ds(0, MAXB, stride=8), :]
                for r in range(1, 8):
                    total_real = total_real + sums[4 * g + 2 * q, pl.ds(r, MAXB, stride=8), :]
                    total_imag = total_imag + sums[4 * g + 2 * q + 1, pl.ds(r, MAXB, stride=8), :]
                cos, sin = turns_to_phase((x * centre_x + y * centre_y) * (1.0 / SG))
                real = real + (cos * total_real + sin * total_imag)
                imag = imag + (cos * total_imag - sin * total_real)
            scale = 1.0 / (math.sqrt(FH) * SG)
            value = (jnp.concatenate([real, imag], axis=0) * scale).astype(BF16)
            out_ref[o, pl.ds(pl.multiple_of(2 * MAXB * c, 2 * MAXB), 2 * MAXB), :] = value


def degrid(plan, own, other, coords, together=TOGETHER):
    smem = pl.BlockSpec(memory_space=pltpu.SMEM)
    vmem = pl.BlockSpec(memory_space=pltpu.VMEM)
    return pl.pallas_call(
        functools.partial(degrid_kernel, together),
        out_shape=jax.ShapeDtypeStruct((16, CAP * 2 * MAXB, VB), BF16),
        in_specs=[smem, vmem, pl.BlockSpec(memory_space=pltpu.HBM), vmem],
        out_specs=vmem,
        scratch_shapes=[
            pltpu.VMEM((4, 16 * CAP, MAXB, VB), F32),
            pltpu.VMEM(((16 * CAP + 1) * 4, 8 * MAXB, VB), F32),
            pltpu.VMEM((S, 2 * W, 2 * W), BF16),
            pltpu.SemaphoreType.DMA,
        ],
        compiler_params=pltpu.CompilerParams(vmem_limit_bytes=VMEM_LIMIT),
        cost_estimate=pl.CostEstimate(flops=12_000_000_000, bytes_accessed=8_000_000, transcendentals=0),
        name="degrid",
    )(plan, own, other, coords)


def jones_kernel(place, stations_ref, table_ref, out_ref, mask_ref):
    pol = place[0]
    row_side, col_side = pol // 2, pol % 2

    def side(which):
        return [
            jnp.where(which == 1, table_ref[4:8, at : at + VB], table_ref[0:4, at : at + VB])
            for at in range(0, 4 * VB, VB)
        ]

    def entry(table, row, station):
        lane, chunk = station % VB, station // VB
        value = jnp.zeros((MAXB, VB), F32)
        for part in range(4):
            line = jnp.broadcast_to(table[part][row : row + 1], (MAXB, VB))
            value = jnp.where(chunk == part, jnp.take_along_axis(line, lane, axis=1), value)
        return value

    left_table, right_table = side(row_side), side(col_side)
    block = lax.broadcasted_iota(jnp.int32, (MAXB, VB), 0)
    for c in range(CAP):
        mask_ref[c] = jnp.where(block < place[1 + c], 1.0, 0.0)
        left, right = stations_ref[c, 0], stations_ref[c, 1]
        lefts = [[entry(left_table, 2 * k + ri, left) for ri in range(2)] for k in range(2)]
        rights = [[entry(right_table, 2 * k + ri, right) for ri in range(2)] for k in range(2)]
        for turn in range(4):
            comp = (pol + 4 - turn) % 4
            left_real, left_imag = (jnp.where(comp // 2 == 1, lefts[1][ri], lefts[0][ri]) for ri in range(2))
            right_real, right_imag = (jnp.where(comp % 2 == 1, rights[1][ri], rights[0][ri]) for ri in range(2))
            out_ref[turn, c, 0] = left_real * right_real + left_imag * right_imag
            out_ref[turn, c, 1] = left_imag * right_real - left_real * right_imag


def jones(place, stations, table):
    smem = pl.BlockSpec(memory_space=pltpu.SMEM)
    vmem = pl.BlockSpec(memory_space=pltpu.VMEM)
    return pl.pallas_call(
        jones_kernel,
        out_shape=[
            jax.ShapeDtypeStruct((4, CAP, 2, MAXB, VB), F32),
            jax.ShapeDtypeStruct((CAP, MAXB, VB), F32),
        ],
        in_specs=[smem, vmem, vmem],
        out_specs=[vmem, vmem],
        compiler_params=pltpu.CompilerParams(vmem_limit_bytes=VMEM_LIMIT),
        name="jones",
    )(place, stations, table)


def correct_kernel(jones_ref, mask_ref, own_ref, one_ref, two_ref, three_ref, out_ref):
    for c in range(CAP):
        total_real = total_imag = jnp.zeros((MAXB, VB), F32)
        for turn, ref in enumerate((own_ref, one_ref, two_ref, three_ref)):
            at = 2 * MAXB * c
            real, imag = ref[at : at + MAXB, :], ref[at + MAXB : at + 2 * MAXB, :]
            step_real, step_imag = jones_ref[turn, c, 0], jones_ref[turn, c, 1]
            total_real = total_real + (step_real * real - step_imag * imag)
            total_imag = total_imag + (step_real * imag + step_imag * real)
        keep = mask_ref[c] > 0.0
        out_ref[0, 0, c] = jnp.where(keep, total_real, 0.0)
        out_ref[0, 1, c] = jnp.where(keep, total_imag, 0.0)


def correct(factors, mask, parts):
    vmem = pl.BlockSpec(memory_space=pltpu.VMEM)
    return pl.pallas_call(
        correct_kernel,
        out_shape=jax.ShapeDtypeStruct((1, 2, CAP, MAXB, VB), F32),
        in_specs=[vmem] * 6,
        out_specs=vmem,
        compiler_params=pltpu.CompilerParams(vmem_limit_bytes=VMEM_LIMIT),
        name="correct",
    )(factors, mask, *parts)


def on_device(facets, owners, counts, coords, station_ids, jones_table):
    chip = lax.axis_index("z") * 4 + lax.axis_index("x")
    core = lax.axis_index("core")
    pol = lax.axis_index("pol")

    own, spread = transform(facets[0], coords.reshape(2 * CAP * MAXB, VB))
    coords_all = lax.all_to_all(spread, ("z", "x"), split_axis=0, concat_axis=0, tiled=True)

    coords_all = coords_all.reshape(16, 2 * CAP, MAXB, VB)

    index = jnp.arange(S, dtype=jnp.int32)
    before = index[None, :] < index[:, None]
    mine = owners % 2 == core
    pairs = jnp.where(mine, (counts + 1) // 2, 0)
    rank = jnp.sum(jnp.where(before & (owners[None, :] == owners[:, None]), 1, 0), axis=1)
    first_unit = jnp.sum(jnp.where(before, pairs[None, :], 0), axis=1)
    slot = (owners // 2) * CAP + rank
    unit_index = jnp.arange(UNITS, dtype=jnp.int32)[:, None]
    offset = unit_index - first_unit[None, :]
    words = (slot * S + index)[None, :] * 4 + offset
    units = jnp.sum(jnp.where((offset >= 0) & (offset < pairs[None, :]), words, 0), axis=1)
    slots = jnp.arange(16 * CAP, dtype=jnp.int32)[:, None]
    place = jnp.sum(jnp.where(before & mine[None, :], 1, 0), axis=1)
    own_slots = jnp.sum(jnp.where((slots == place[None, :]) & mine[None, :], slot[None, :], 0), axis=1)
    facet = 2 * (chip * 2 + core)
    extra = jnp.stack([jnp.sum(pairs), facet, facet + 2 - 4 * core, jnp.sum(jnp.where(mine, 1, 0))])
    plan = jnp.concatenate([units, own_slots, extra, jnp.zeros((60,), jnp.int32)])
    own_limits = jnp.sum(
        jnp.where((slot[None, :] == chip * CAP + jnp.arange(CAP)[:, None]) & mine[None, :], counts[None, :], 0), axis=1
    )

    other = lax.ppermute(own, "core", [(0, 1), (1, 0)])
    parts = degrid(plan, own, other, coords_all)
    parts = lax.all_to_all(parts, ("z", "x"), split_axis=0, concat_axis=0, tiled=True)
    visible = jnp.sum(parts.astype(F32), axis=0)
    place = jnp.concatenate([pol.reshape(1), own_limits]).astype(jnp.int32)
    factors, mask = jones(place, jnp.moveaxis(station_ids, 2, 1), jones_table)
    turns = [lax.ppermute(visible, "pol", [(i, (i + k) % 4) for i in range(4)]) for k in (1, 2, 3)]
    return correct(factors, mask, [visible] + turns)


def solution(mesh):
    split = jax.sharding.Mesh(mesh.devices.reshape(4, 4, 2, 4), ("z", "x", "core", "pol"))
    fs = ("z", "x", "core")
    return jax.shard_map(
        on_device,
        mesh=split,
        in_specs=(P("pol", fs, None, None), P(), P(), P(None, fs, None, None), P(fs, None, None, None), P()),
        out_specs=P("pol", None, fs, None, None),
        check_vma=False,
    )
```

```python
import functools
import math

import jax
import jax.numpy as jnp
import numpy as np
from jax import lax
from jax.experimental import pallas as pl
from jax.experimental.pallas import tpu as pltpu
from jax.sharding import PartitionSpec as P

R = 8
W = 64
S = 64
MAXB = 8
VB = 128
FH = 4096
SG = 512
CAP = 4
UNITS = 256
TOTAL_AT = UNITS + 64
GROUP = 16
TOGETHER = 8
VMEM_LIMIT = 48 * 1024 * 1024
F32 = jnp.float32
BF16 = jnp.bfloat16


def first_table():
    index = np.arange(W)
    angles = (index[:, None] * index[None, :] % W) * (2.0 * math.pi / W)
    waves = np.concatenate([np.cos(angles[: W // 2 + 1]), np.sin(angles[1 : W // 2])], axis=0)
    return np.repeat(waves, GROUP, axis=1).astype(BF16)


def second_table():
    k1 = np.arange(W)[:, None, None]
    k2 = np.arange(S)[None, :, None]
    n1 = np.arange(W)[None, None, :]
    angles = (n1 * (k1 + W * k2) % FH) * (2.0 * math.pi / FH)
    cos, sin = np.cos(angles), np.sin(angles)
    sign = np.where(k1 % (W // 2) == 0, 0.0, np.where(k1 < W // 2, 1.0, -1.0))
    upper = np.concatenate([cos, -sin * sign], axis=2)
    lower = np.concatenate([sin, cos * sign], axis=2)
    return np.concatenate([upper, lower], axis=1).astype(BF16)


SIN_TERMS = (3.14159264, -5.16771008, 2.55007752, -0.598291286, 0.0776576603)
COS_TERMS = (0.999999953, -4.93479283, 4.05841135, -1.33187657, 0.219689611)


def polynomial(terms, x):
    total = jnp.full_like(x, terms[-1])
    for term in terms[-2::-1]:
        total = total * x + term
    return total


def turns_to_phase(turns):
    part = turns - jnp.round(turns)
    square = part * part
    half_sin = part * polynomial(SIN_TERMS, square)
    half_cos = polynomial(COS_TERMS, square)
    twice = half_sin + half_sin
    return (1.0 - twice * half_sin, twice * half_cos)


def rotate(cos, sin, step_cos, step_sin):
    return (cos * step_cos - sin * step_sin, sin * step_cos + cos * step_sin)


def transform_kernel(
    facets_hbm, waves_hbm, second_hbm, out_ref, facets_ref, waves_ref, second_ref, first_ref, sections, mixed, sems
):
    half = W // 2
    wide = W * GROUP
    waves_copy = pltpu.make_async_copy(waves_hbm, waves_ref, sems.at[4])
    quarters = [pl.ds(16 * i, 16) for i in range(4)]
    second_copies = [
        pltpu.make_async_copy(second_hbm.at[at], second_ref.at[at], sems.at[i]) for i, at in enumerate(quarters)
    ]
    strip_copies = [
        pltpu.make_async_copy(facets_hbm.at[f, at], facets_ref.at[f, at], sems.at[5 + 4 * f + i])
        for f in range(2)
        for i, at in enumerate(quarters)
    ]
    for copy in [waves_copy] + strip_copies + second_copies:
        copy.start()
    row = lax.broadcasted_iota(jnp.int32, (2 * W, 2 * W), 0)
    lane = lax.broadcasted_iota(jnp.int32, (2 * W, 2 * W), 1)
    mirror = jnp.where(row == jnp.where(lane < W, W - 1, 3 * W - 1) - lane, 1.0, 0.0).astype(BF16)

    pieces = [slice(piece * 256, piece * 256 + 256) for piece in range(4)]
    cell = lax.broadcasted_iota(jnp.int32, (256, wide), 0) & (GROUP - 1)
    same = cell == (lax.broadcasted_iota(jnp.int32, (256, wide), 1) & (GROUP - 1))
    wave = lax.broadcasted_iota(jnp.int32, (256, W), 1)
    line = lax.broadcasted_iota(jnp.int32, (256, W), 0) >> 4
    waves_copy.wait()
    for piece, rows in enumerate(pieces):
        pick = jnp.where(line + 16 * piece == wave, 1.0, 0.0).astype(BF16)
        spread_waves = jnp.dot(pick, waves_ref[...], preferred_element_type=F32)
        first_ref[rows, :] = jnp.where(same, spread_waves, 0.0).astype(BF16)

    for copy in strip_copies:
        copy.wait()
    for h in range(W // GROUP):
        at = slice(GROUP * h, GROUP * h + GROUP)
        strip = [facets_ref[f, :, at, :].reshape(wide, 2 * W) for f in range(2)]
        mirrored = jnp.dot(strip[0], mirror, preferred_element_type=F32).astype(BF16)
        strips = jnp.concatenate([mirrored, strip[1]], axis=1)
        for piece, rows in enumerate(pieces):
            part = jnp.dot(first_ref[rows, :], strips, preferred_element_type=F32).astype(BF16)
            for f in range(2):
                block = part[:, 2 * W * f : 2 * W * (f + 1)].reshape(16, GROUP, 2 * W)
                sections[f, piece * 16 : piece * 16 + 16, at, :] = block
    for copy in second_copies:
        copy.wait()

    low_lanes = lax.broadcasted_iota(jnp.int32, (S, 2 * W), 1) < W

    def window(k1, fold):
        section = jnp.concatenate(
            [
                jnp.concatenate([sections[f, fold], sections[f, min(half + fold, W - 1)]], axis=0)
                for f in range(2)
            ],
            axis=1,
        )
        return jnp.dot(second_ref[k1], section, preferred_element_type=F32)

    for index in range(half):
        above = window(half + index, half - index)
        below = window(half - 1 - index, half - 1 - index)
        for pick, grid in enumerate((above + below, above - below)):
            cos_0, cos_1 = grid[:S, : 2 * W], grid[:S, 2 * W :]
            sin_0, sin_1 = grid[S:, : 2 * W], grid[S:, 2 * W :]
            cos_sum, cos_gap = cos_1 + cos_0, cos_1 - cos_0
            sin_sum, sin_gap = sin_1 + sin_0, sin_1 - sin_0
            real = jnp.where(low_lanes, cos_sum, cos_gap) + pltpu.roll(
                jnp.where(low_lanes, -sin_gap, sin_sum), W, 1
            )
            imag = pltpu.roll(jnp.where(low_lanes, -cos_gap, cos_sum), W, 1) - jnp.where(
                low_lanes, sin_sum, sin_gap
            )
            mixed[2 * pick, index] = real
            mixed[2 * pick + 1, index] = imag

    @pl.loop(0, S // 8)
    def _(step):
        at = pl.ds(pl.multiple_of(step * 8, 8), 8)
        for kind in range(4):
            for i in range(0, half, 16):
                halves = [jnp.swapaxes(mixed[kind, i + j : i + j + 8, at, :], 0, 1) for j in (0, 8)]
                rows = slice(half * kind + i, half * kind + i + 16)
                out_ref[at, rows, :] = jnp.concatenate(halves, axis=1).astype(BF16)


def spread_kernel(coords_ref, out_hbm, sems):
    copies = [pltpu.make_async_copy(coords_ref, out_hbm.at[o], sems.at[o]) for o in range(16)]
    for copy in copies:
        copy.start()
    for copy in copies:
        copy.wait()


def spread(coords):
    return pl.pallas_call(
        spread_kernel,
        out_shape=jax.ShapeDtypeStruct((16,) + coords.shape, F32),
        in_specs=[pl.BlockSpec(memory_space=pltpu.VMEM)],
        out_specs=pl.BlockSpec(memory_space=pltpu.HBM),
        scratch_shapes=[pltpu.SemaphoreType.DMA((16,))],
        name="spread",
    )(coords)


def in_hbm(array):
    return pltpu.with_memory_space_constraint(array, pltpu.HBM)


def transform(strips):
    return pl.pallas_call(
        transform_kernel,
        out_shape=jax.ShapeDtypeStruct((S, 2 * W, 2 * W), BF16),
        in_specs=[pl.BlockSpec(memory_space=pltpu.HBM)] * 3,
        out_specs=pl.BlockSpec(memory_space=pltpu.VMEM),
        scratch_shapes=[
            pltpu.VMEM((2, W, W, 2 * W), BF16),
            pltpu.VMEM((W, W * GROUP), BF16),
            pltpu.VMEM((W, 2 * W, 2 * W), BF16),
            pltpu.VMEM((W * GROUP, W * GROUP), BF16),
            pltpu.VMEM((2, W, W, 2 * W), BF16),
            pltpu.VMEM((4, W // 2, S, 2 * W), F32),
            pltpu.SemaphoreType.DMA((13,)),
        ],
        compiler_params=pltpu.CompilerParams(vmem_limit_bytes=VMEM_LIMIT),
        cost_estimate=pl.CostEstimate(flops=12_000_000_000, bytes_accessed=8_000_000, transcendentals=0),
        name="transform",
    )(*(in_hbm(x) for x in (strips.reshape(2, W, W, 2 * W), jnp.asarray(first_table()), jnp.asarray(second_table()))))


def degrid_kernel(together, plan, own_ref, other_hbm, coords_ref, out_ref, steps, sums, other_ref, sem):
    other_copy = pltpu.make_async_copy(other_hbm, other_ref, sem)
    other_copy.start()

    rounds = (plan[TOTAL_AT + 3] + 3) >> 2

    @pl.loop(0, rounds)
    def _(step):
        for j in range(4):
            g = plan[UNITS + 4 * step + j]
            for axis in range(2):
                cos, sin = turns_to_phase(coords_ref[g >> 2, CAP * axis + (g & 3)] * (8.0 / SG))
                steps[2 * axis, g] = cos
                steps[2 * axis + 1, g] = sin

    other_copy.wait()
    cells = (lax.broadcasted_iota(jnp.int32, (8, VB), 0).astype(F32) + 0.5) * (1.0 / SG)

    def ladder(position, step_cos, step_sin, count):
        cos, sin = turns_to_phase(position * cells)
        both = [(cos, sin)]
        step_cos = jnp.broadcast_to(step_cos, (8, VB))
        step_sin = jnp.broadcast_to(step_sin, (8, VB))
        both.append(rotate(cos, sin, step_cos, step_sin))
        twice = step_cos + step_cos
        while len(both) < count:
            both.append(tuple(twice * last - first for first, last in zip(*both[-2:])))
        return both

    def place(index):
        word = plan[index]
        g = word >> 8
        kept = jnp.where(index < plan[TOTAL_AT], g, 16 * CAP)
        return (g >> 2, g & 3, g, kept, (word >> 2) & (S - 1), (word & 3) << 1)

    def phases_of(o, c, g, kept, s, b):
        blocks = []
        for h in range(2):
            row = pl.ds(b + h, 1)
            along = ladder(coords_ref[o, CAP + c, row, :], steps[2, g, row, :], steps[3, g, row, :], 8)
            blocks.append(jnp.concatenate([t[0] for t in along] + [t[1] for t in along], axis=0).astype(BF16))
        return jnp.concatenate(blocks, axis=1)

    def finish(grid, o, c, g, kept, s, b):
        for h in range(2):
            row = pl.ds(b + h, 1)
            lanes = slice(VB * h, VB * (h + 1))
            weights = ladder(coords_ref[o, c, row, :], steps[0, g, row, :], steps[1, g, row, :], 4)
            for q in range(2):
                real = imag = None
                for i, (cos, sin) in enumerate(weights):
                    at = 128 * q + 8 * i
                    sum_real, sum_imag = grid[at : at + 8, lanes], grid[at + 32 : at + 40, lanes]
                    gap_real, gap_imag = grid[at + 64 : at + 72, lanes], grid[at + 96 : at + 104, lanes]
                    step_real = cos * sum_real + sin * gap_imag
                    step_imag = cos * sum_imag - sin * gap_real
                    real = step_real if real is None else real + step_real
                    imag = step_imag if imag is None else imag + step_imag
                at = pl.ds(pl.multiple_of(8 * (b + h), 8), 8)
                sums[4 * kept + 2 * q, at, :] = real
                sums[4 * kept + 2 * q + 1, at, :] = imag

    @pl.loop(0, (plan[TOTAL_AT] + together - 1) // together)
    def _(step):
        at = [place(step * together + j) for j in range(together)]
        phases = [phases_of(*a) for a in at]
        grids = []
        for a, p in zip(at, phases):
            both = jnp.concatenate([own_ref[a[4]], other_ref[a[4]]], axis=0)
            grids.append(jnp.dot(both, p, preferred_element_type=F32))
        for a, grid in zip(at, grids):
            finish(grid, *a)

    first_facet, other_facet = plan[TOTAL_AT + 1], plan[TOTAL_AT + 2]
    centre_x = (W * (first_facet // R)).astype(F32) + (W // 2 - 0.5 - SG // 2)
    centre_own = (W * (first_facet % R)).astype(F32) + (W - 0.5 - SG // 2)
    centre_other = (W * (other_facet % R)).astype(F32) + (W - 0.5 - SG // 2)

    @pl.loop(0, rounds)
    def _(step):
        for j in range(4):
            g = plan[UNITS + 4 * step + j]
            o, c = g >> 2, g & 3
            x, y = coords_ref[o, c], coords_ref[o, CAP + c]
            real = imag = jnp.zeros((MAXB, VB), F32)
            for q, centre_y in enumerate((centre_own, centre_other)):
                total_real = sums[4 * g + 2 * q, pl.ds(0, MAXB, stride=8), :]
                total_imag = sums[4 * g + 2 * q + 1, pl.ds(0, MAXB, stride=8), :]
                for r in range(1, 8):
                    total_real = total_real + sums[4 * g + 2 * q, pl.ds(r, MAXB, stride=8), :]
                    total_imag = total_imag + sums[4 * g + 2 * q + 1, pl.ds(r, MAXB, stride=8), :]
                cos, sin = turns_to_phase((x * centre_x + y * centre_y) * (1.0 / SG))
                real = real + (cos * total_real + sin * total_imag)
                imag = imag + (cos * total_imag - sin * total_real)
            scale = 1.0 / (math.sqrt(FH) * SG)
            value = (jnp.concatenate([real, imag], axis=0) * scale).astype(BF16)
            out_ref[o, pl.ds(pl.multiple_of(2 * MAXB * c, 2 * MAXB), 2 * MAXB), :] = value


def degrid(plan, own, other, coords, together=TOGETHER):
    smem = pl.BlockSpec(memory_space=pltpu.SMEM)
    vmem = pl.BlockSpec(memory_space=pltpu.VMEM)
    return pl.pallas_call(
        functools.partial(degrid_kernel, together),
        out_shape=jax.ShapeDtypeStruct((16, CAP * 2 * MAXB, VB), BF16),
        in_specs=[smem, vmem, pl.BlockSpec(memory_space=pltpu.HBM), vmem],
        out_specs=vmem,
        scratch_shapes=[
            pltpu.VMEM((4, 16 * CAP, MAXB, VB), F32),
            pltpu.VMEM(((16 * CAP + 1) * 4, 8 * MAXB, VB), F32),
            pltpu.VMEM((S, 2 * W, 2 * W), BF16),
            pltpu.SemaphoreType.DMA,
        ],
        compiler_params=pltpu.CompilerParams(vmem_limit_bytes=VMEM_LIMIT),
        cost_estimate=pl.CostEstimate(flops=12_000_000_000, bytes_accessed=8_000_000, transcendentals=0),
        name="degrid",
    )(plan, own, other, coords)


def jones_kernel(place, stations_ref, table_ref, out_ref, mask_ref):
    pol = place[0]
    row_side, col_side = pol // 2, pol % 2

    def side(which):
        return [
            jnp.where(which == 1, table_ref[4:8, at : at + VB], table_ref[0:4, at : at + VB])
            for at in range(0, 4 * VB, VB)
        ]

    def entry(table, row, station):
        lane, chunk = station % VB, station // VB
        value = jnp.zeros((MAXB, VB), F32)
        for part in range(4):
            line = jnp.broadcast_to(table[part][row : row + 1], (MAXB, VB))
            value = jnp.where(chunk == part, jnp.take_along_axis(line, lane, axis=1), value)
        return value

    left_table, right_table = side(row_side), side(col_side)
    block = lax.broadcasted_iota(jnp.int32, (MAXB, VB), 0)
    for c in range(CAP):
        mask_ref[c] = jnp.where(block < place[1 + c], 1.0, 0.0)
        left, right = stations_ref[c, 0], stations_ref[c, 1]
        lefts = [[entry(left_table, 2 * k + ri, left) for ri in range(2)] for k in range(2)]
        rights = [[entry(right_table, 2 * k + ri, right) for ri in range(2)] for k in range(2)]
        for turn in range(4):
            comp = (pol + 4 - turn) % 4
            left_real, left_imag = (jnp.where(comp // 2 == 1, lefts[1][ri], lefts[0][ri]) for ri in range(2))
            right_real, right_imag = (jnp.where(comp % 2 == 1, rights[1][ri], rights[0][ri]) for ri in range(2))
            out_ref[turn, c, 0] = left_real * right_real + left_imag * right_imag
            out_ref[turn, c, 1] = left_imag * right_real - left_real * right_imag


def jones(place, stations, table):
    smem = pl.BlockSpec(memory_space=pltpu.SMEM)
    vmem = pl.BlockSpec(memory_space=pltpu.VMEM)
    return pl.pallas_call(
        jones_kernel,
        out_shape=[
            jax.ShapeDtypeStruct((4, CAP, 2, MAXB, VB), F32),
            jax.ShapeDtypeStruct((CAP, MAXB, VB), F32),
        ],
        in_specs=[smem, vmem, vmem],
        out_specs=[vmem, vmem],
        compiler_params=pltpu.CompilerParams(vmem_limit_bytes=VMEM_LIMIT),
        name="jones",
    )(place, stations, table)


def correct_kernel(jones_ref, mask_ref, own_ref, one_ref, two_ref, three_ref, out_ref):
    for c in range(CAP):
        total_real = total_imag = jnp.zeros((MAXB, VB), F32)
        for turn, ref in enumerate((own_ref, one_ref, two_ref, three_ref)):
            at = 2 * MAXB * c
            real, imag = ref[at : at + MAXB, :], ref[at + MAXB : at + 2 * MAXB, :]
            step_real, step_imag = jones_ref[turn, c, 0], jones_ref[turn, c, 1]
            total_real = total_real + (step_real * real - step_imag * imag)
            total_imag = total_imag + (step_real * imag + step_imag * real)
        keep = mask_ref[c] > 0.0
        out_ref[0, 0, c] = jnp.where(keep, total_real, 0.0)
        out_ref[0, 1, c] = jnp.where(keep, total_imag, 0.0)


def correct(factors, mask, parts):
    vmem = pl.BlockSpec(memory_space=pltpu.VMEM)
    return pl.pallas_call(
        correct_kernel,
        out_shape=jax.ShapeDtypeStruct((1, 2, CAP, MAXB, VB), F32),
        in_specs=[vmem] * 6,
        out_specs=vmem,
        compiler_params=pltpu.CompilerParams(vmem_limit_bytes=VMEM_LIMIT),
        name="correct",
    )(factors, mask, *parts)


def on_device(facets, owners, counts, coords, station_ids, jones_table):
    chip = lax.axis_index("z") * 4 + lax.axis_index("x")
    core = lax.axis_index("core")
    pol = lax.axis_index("pol")

    coords_all = lax.all_to_all(spread(coords.reshape(2 * CAP * MAXB, VB)), ("z", "x"), split_axis=0, concat_axis=0, tiled=True)

    coords_all = coords_all.reshape(16, 2 * CAP, MAXB, VB)

    index = jnp.arange(S, dtype=jnp.int32)
    before = index[None, :] < index[:, None]
    mine = owners % 2 == core
    pairs = jnp.where(mine, (counts + 1) // 2, 0)
    rank = jnp.sum(jnp.where(before & (owners[None, :] == owners[:, None]), 1, 0), axis=1)
    first_unit = jnp.sum(jnp.where(before, pairs[None, :], 0), axis=1)
    slot = (owners // 2) * CAP + rank
    unit_index = jnp.arange(UNITS, dtype=jnp.int32)[:, None]
    offset = unit_index - first_unit[None, :]
    words = (slot * S + index)[None, :] * 4 + offset
    units = jnp.sum(jnp.where((offset >= 0) & (offset < pairs[None, :]), words, 0), axis=1)
    slots = jnp.arange(16 * CAP, dtype=jnp.int32)[:, None]
    place = jnp.sum(jnp.where(before & mine[None, :], 1, 0), axis=1)
    own_slots = jnp.sum(jnp.where((slots == place[None, :]) & mine[None, :], slot[None, :], 0), axis=1)
    facet = 2 * (chip * 2 + core)
    extra = jnp.stack([jnp.sum(pairs), facet, facet + 2 - 4 * core, jnp.sum(jnp.where(mine, 1, 0))])
    plan = jnp.concatenate([units, own_slots, extra, jnp.zeros((60,), jnp.int32)])
    own_limits = jnp.sum(
        jnp.where((slot[None, :] == chip * CAP + jnp.arange(CAP)[:, None]) & mine[None, :], counts[None, :], 0), axis=1
    )

    own = transform(facets[0])
    sent, coords_all = lax.optimization_barrier((own, coords_all))
    other = lax.ppermute(sent, "core", [(0, 1), (1, 0)])
    parts = degrid(plan, own, other, coords_all)
    parts = lax.all_to_all(parts, ("z", "x"), split_axis=0, concat_axis=0, tiled=True)
    visible = jnp.sum(parts.astype(F32), axis=0)
    place = jnp.concatenate([pol.reshape(1), own_limits]).astype(jnp.int32)
    factors, mask = jones(place, jnp.moveaxis(station_ids, 2, 1), jones_table)
    turns = [lax.ppermute(visible, "pol", [(i, (i + k) % 4) for i in range(4)]) for k in (1, 2, 3)]
    return correct(factors, mask, [visible] + turns)


def solution(mesh):
    split = jax.sharding.Mesh(mesh.devices.reshape(4, 4, 2, 4), ("z", "x", "core", "pol"))
    fs = ("z", "x", "core")
    return jax.shard_map(
        on_device,
        mesh=split,
        in_specs=(P("pol", fs, None, None), P(), P(), P(None, fs, None, None), P(fs, None, None, None), P()),
        out_specs=P("pol", None, fs, None, None),
        check_vma=False,
    )
```
